512 devices in a mesh: exp: 64 (over x, y, core), rep: 8 (over z).
Axes of the slice: x: 4, y: 8, z: 8, core: 2. Of those that a mesh axis runs over, the one named last changes fastest.
Arguments:
- passages_in: bfloat16 [92160, 2048], P(('exp', 'rep')), may hold values from -24 to 32
- routes: int32 [92160, 2], P(('exp', 'rep')), may hold values from 0 to 63, all different within a row; in each aligned block of 180 rows (0 to 179, 180 to 359, ...) at most 11 rows name the same one
- route_weights: float32 [92160, 2], P(('exp', 'rep')), may hold values from 0.2 to 1
- gate_weight: bfloat16 [64, 2048, 704], P('exp', 'rep'), may hold values from -0.125 to 0.125
- up_weight: bfloat16 [64, 2048, 704], P('exp', 'rep'), may hold values from -0.125 to 0.125
- down_weight: bfloat16 [64, 704, 2048], P('exp', None, 'rep'), may hold values from -0.21875 to 0.21875
- projection: bfloat16 [2048, 128], replicated, may hold values from -2 to 2
- queries: bfloat16 [128, 32, 128], P('rep'), may hold values from -6 to 6
- positives: int32 [128], replicated, may hold values from 0 to 511, as said below
Outputs:
- states: bfloat16 [92160, 2048], P(('exp', 'rep'))
- grad_projection: float32 [2048, 128], P('exp')
- mean_loss: float32 [], replicated
The draws below stay inside these ranges and needn't reach their ends.
Inputs may be any that keep to these rules, and one draw needn't show every extreme that they name: `routes`: the two experts of a token differ. Among the rows of one device, no expert is named more than 11 times, and in some device's rows some expert is named exactly 11 times; every expert is named somewhere. `positives`: distinct queries have distinct positive passages.
All inputs are finite; a program needn't handle non-finite values.
Results may differ from the reference program's by a relative error of at most 0.0065.
Values may be sent and summed in bfloat16 or wider, within the bound.
No kernel may reach another device: no remote copies, remote signals or barrier semaphores. Data moves between devices by JAX's collectives and lax.ppermute only.
A program may use at most 64 MiB of HBM per device.

```python
import math
import jax
import jax.numpy as jnp
import numpy as np
from jax import lax

D = 2048
FF = 704
DIM = 128
TOP = 2
PAS_LEN = 180
QLEN = 32
EXPERTS = 64
TOK_DEV = 180
CAP = 11
TOKENS = 92160
PASSAGES = 512
QUERIES = 128
N_EXP = 64
N_REP = 8
DEVICES = 512


plant_gain = 6.0


plant_reach = 1.3


def drawn_rows():
    return max(1, min(8, D // (2 * QUERIES)))


def pick_targets(key):
    key = jax.random.fold_in(key, 101)
    passage_key, row_key = jax.random.split(key)
    chosen = jax.random.permutation(passage_key, PASSAGES)[:QUERIES].astype(jnp.int32)
    row_count = drawn_rows()
    rows = jax.random.permutation(row_key, D)[:QUERIES * row_count].astype(jnp.int32).reshape(QUERIES, row_count)
    return (chosen, rows)


def pick_directions(key):
    key = jax.random.fold_in(key, 202)
    return jnp.clip(jax.random.normal(key, (QUERIES, DIM), jnp.float32), -3.0, 3.0)


def draw_passages_in(key, part):
    chosen, rows = pick_targets(key)
    key = jax.random.fold_in(key, 3)
    noise_key, pair_key, amp_key = jax.random.split(key, 3)
    noise = jnp.clip(jax.random.normal(noise_key, (TOKENS, D), jnp.float32), -6.0, 6.0)
    width = max(1, D // DEVICES)
    blocks = D // width
    pairing = jax.random.permutation(pair_key, DEVICES).astype(jnp.int32) % blocks
    device_of = jnp.arange(TOKENS, dtype=jnp.int32) // TOK_DEV
    column_block = jnp.arange(D, dtype=jnp.int32) // width
    boosted = column_block[None, :] == pairing[device_of][:, None]
    noise = jnp.where(boosted, 4.0 * noise, noise)
    row_table = jnp.zeros((QUERIES, D), jnp.float32).at[jnp.arange(QUERIES, dtype=jnp.int32)[:, None], rows].set(1.0)
    owner_table = jnp.zeros((PASSAGES, D), jnp.float32).at[chosen].set(row_table)
    amplitude = plant_gain * jax.random.uniform(amp_key, (PASSAGES, PAS_LEN, 1), jnp.float32, 0.75, 1.25)
    planted = (owner_table[:, None, :] * amplitude).reshape(TOKENS, D)
    return (noise + planted).astype(jnp.bfloat16)


def draw_projection(key, part):
    chosen, rows = pick_targets(key)
    directions = pick_directions(key)
    key = jax.random.fold_in(key, 5)
    base = jnp.clip(jax.random.normal(key, (D, DIM), jnp.float32), -4.0, 4.0)
    base = base * D ** (-0.5)
    row_count = drawn_rows()
    reach = plant_reach / (plant_gain * row_count)
    return base.at[rows.reshape(-1)].add(reach * jnp.repeat(directions, row_count, axis=0)).astype(jnp.bfloat16)


def draw_queries(key, part):
    directions = pick_directions(key)
    key = jax.random.fold_in(key, 7)
    noise_key, margin_key = jax.random.split(key)
    noise = jnp.clip(jax.random.normal(noise_key, (QUERIES, QLEN, DIM), jnp.float32), -5.0, 5.0)
    margin = jax.random.uniform(margin_key, (QUERIES, 1, 1), jnp.float32, 3.0, 7.0)
    return (noise + margin / QLEN * directions[:, None, :]).astype(jnp.bfloat16)


def draw_positives(key, part):
    chosen, rows = pick_targets(key)
    return chosen


def level_of(own_key, shape, shards, least, largest):
    level = 1.0
    for axis_at, shards_of in shards:
        heights = jax.random.uniform(jax.random.fold_in(jax.random.fold_in(own_key, 6), axis_at), (shards_of,), jnp.float32, least / len(shards), largest / len(shards))
        level = level * jnp.repeat(jnp.exp(heights), shape[axis_at] // shards_of).reshape((-1,) + (1,) * (len(shape) - 1 - axis_at))
    return level


def routed_block(key, own, number, rows, number_of, top, most, slope):
    sequence = jax.random.permutation(key, number_of)
    packed, ordinary = shares(number_of, rows * top, most, slope, True), shares(number_of, rows * top, most, slope, False)
    places = jnp.arange(number_of)

    def named(lengths, offset_by):
        used = int((lengths > 0).sum())
        fixed = max(1, used // 4)
        shifted = fixed + (places - fixed + offset_by * (used - fixed)) % max(1, number_of - fixed)
        return jnp.zeros((number_of,), jnp.int32).at[sequence[jnp.where(places < fixed, places, shifted)]].set(jnp.asarray(lengths, jnp.int32))

    lengths = jnp.where(number % 4 == 0, named(packed, number // 4), named(ordinary, number - number // 4 - 1))
    mixed = jax.random.permutation(jax.random.fold_in(own, 3), number_of)
    donor, receiver = mixed[0:number_of // 2 * 2:2], mixed[1:number_of // 2 * 2:2]
    room = jnp.minimum(lengths[donor] - 1, most - lengths[receiver]) // 2
    room = jnp.where((donor == sequence[0]) | (receiver == sequence[0]) | (lengths[receiver] == 0), 0, jnp.maximum(room, 0))
    shifted = jax.random.randint(jax.random.fold_in(own, 4), (number_of // 2,), 0, 1 << 20) % (room + 1)
    lengths = lengths.at[donor].add(-shifted).at[receiver].add(shifted)
    members = jnp.searchsorted(jnp.cumsum(lengths), jnp.arange(rows * top), side="right").astype(jnp.int32)
    grid = members.reshape(top, rows).T
    grid = grid[jax.random.permutation(jax.random.fold_in(own, 1), rows)]
    offset_by = jax.random.randint(jax.random.fold_in(own, 2), (rows, 1), 0, top)
    return jnp.take_along_axis(grid, (jnp.arange(top)[None, :] + offset_by) % top, axis=1)


def shares(number_of, total, most, skew, full):
    weights = [(1 << 20) // math.isqrt(standing ** skew) + 1 for standing in range(1, number_of + 1)]
    largest = most if full else min(most, max(-(-total // number_of), total * weights[0] // sum(weights)))
    least = 1 if total - largest >= number_of - 1 else 0
    counts, rest = [largest] + [least] * (number_of - 1), total - largest - least * (number_of - 1)
    while rest > 0:
        free = [i for i in range(1, number_of) if counts[i] < largest] or [i for i in range(1, number_of) if counts[i] < most]
        mass, budget = sum([weights[i] for i in free]), rest
        for i in free:
            extra = min(most - counts[i], max(1, budget * weights[i] // mass), rest)
            counts[i] = counts[i] + extra
            rest = rest - extra
    return np.array(counts)


def normal_values(key, extent, scale, limit, pieces=(), held_as=jnp.bfloat16):
    loudness = level_of(key, extent, pieces, -0.22, 0.18) if pieces else 1.0
    values = jax.random.normal(key, extent, jnp.float32) * scale * loudness
    return jnp.minimum(jnp.maximum(values, -limit), limit).astype(held_as)


def setup_inputs(seed: int = 0) -> dict:
    splits = jax.random.split(jax.random.key(seed), 10)
    passages_in = draw_passages_in(jax.random.fold_in(splits[9], 71), 0)
    routes_keys = jax.random.split(jax.random.fold_in(splits[1], 1), TOKENS // TOK_DEV)
    routes_turns = jax.random.permutation(jax.random.fold_in(splits[1], 3), TOKENS // TOK_DEV)
    routes = jax.vmap(lambda own, number: routed_block(jax.random.fold_in(splits[1], 2), own, number, TOK_DEV, EXPERTS, TOP, CAP, 2))(routes_keys, routes_turns).reshape((TOKENS, TOP))
    route_weights = jnp.clip(0.2 + 0.8 * jax.random.uniform(splits[2], (TOKENS, TOP), jnp.float32) ** level_of(splits[2], (TOKENS, TOP), ((0, 512),), -0.2, 0.2), 0.2, 1.0)
    gate_weight = normal_values(splits[3], (EXPERTS, D, FF), D ** -0.5, 0.125, ((0, 64), (1, 8)))
    up_weight = normal_values(splits[4], (EXPERTS, D, FF), D ** -0.5, 0.125, ((0, 64), (1, 8)))
    down_weight = normal_values(splits[5], (EXPERTS, FF, D), FF ** -0.5, 0.21875, ((0, 64), (2, 8)))
    projection = draw_projection(jax.random.fold_in(splits[9], 71), 0)
    queries = draw_queries(jax.random.fold_in(splits[9], 71), 0)
    positives = draw_positives(jax.random.fold_in(splits[9], 71), 0)
    return {"passages_in": passages_in, "routes": routes, "route_weights": route_weights, "gate_weight": gate_weight, "up_weight": up_weight, "down_weight": down_weight, "projection": projection, "queries": queries, "positives": positives}


soft_temp = 0.05
logit_gain = 1.5
norm_eps = 1e-06

def unit_rows(values):
    values = values.astype(jnp.float32)
    radius = jnp.sqrt(lax.optimization_barrier(jnp.sum(values * values, axis=-1, keepdims=True)) + norm_eps)
    return (values / radius, radius)

def reference(passages_in, routes, route_weights, gate_weight, up_weight, down_weight, projection, queries, positives):
    devices_all = N_EXP * N_REP
    slot_total = devices_all * CAP
    per_device = routes.reshape(devices_all, TOK_DEV * TOP)
    onehot = (per_device[:, :, None] == jnp.arange(EXPERTS, dtype=jnp.int32)[None, None, :]).astype(jnp.int32)
    slot_rank = lax.optimization_barrier(jnp.sum((jnp.cumsum(onehot, axis=1) - onehot) * onehot, axis=2))
    device_ids = jnp.arange(devices_all, dtype=jnp.int32)[:, None]
    places = (per_device * slot_total + device_ids * CAP + slot_rank).reshape(-1)
    token_ids = (device_ids * TOK_DEV + jnp.arange(TOK_DEV * TOP, dtype=jnp.int32)[None, :] // TOP).reshape(-1)
    table = jnp.zeros((EXPERTS * slot_total,), jnp.int32).at[places].set(token_ids).reshape(EXPERTS, slot_total)
    scales = jnp.zeros((EXPERTS * slot_total,), jnp.float32).at[places].set(route_weights.reshape(-1)).reshape(EXPERTS, slot_total)

    def expert_step(running, items):
        row_index, row_scale, w_gate, w_up, w_down = items
        rows = passages_in[row_index]
        gate_sum = jnp.dot(rows, w_gate, preferred_element_type=jnp.float32)
        up_sum = jnp.dot(rows, w_up, preferred_element_type=jnp.float32)
        hidden = (jax.nn.silu(gate_sum) * up_sum).astype(jnp.bfloat16)
        outputs = jnp.dot(hidden, w_down, preferred_element_type=jnp.float32).astype(jnp.bfloat16)
        running = running.at[row_index].add(row_scale[:, None] * outputs.astype(jnp.float32))
        return (running, None)
    running, _ = lax.scan(expert_step, jnp.zeros((TOKENS, D), jnp.float32), (table, scales, gate_weight, up_weight, down_weight))
    states = (passages_in.astype(jnp.float32) + running).astype(jnp.bfloat16)
    projected = jnp.dot(states, projection, preferred_element_type=jnp.float32)
    unit_f32, radius = unit_rows(projected)
    unit_vec = unit_f32.astype(jnp.bfloat16).reshape(PASSAGES, PAS_LEN, DIM)
    query_rows = unit_rows(queries)[0].astype(jnp.bfloat16).reshape(QUERIES * QLEN, DIM)

    def passage_weights(block):
        scores = lax.dot_general(block, query_rows, (((1,), (1,)), ((), ())), preferred_element_type=jnp.float32)
        return jnp.exp(scores / soft_temp)

    def passage_scores(block):
        weights = passage_weights(block)
        totals = lax.optimization_barrier(jnp.sum(weights, axis=0))
        logits = logit_gain * lax.optimization_barrier(jnp.sum((soft_temp * jnp.log(totals)).reshape(QUERIES, QLEN), axis=1))
        return (totals, logits)
    totals, logits = lax.map(passage_scores, unit_vec)
    positive_hit = jnp.arange(PASSAGES, dtype=jnp.int32)[:, None] == positives[None, :]
    exp_logits = jnp.exp(logits)
    partition = lax.optimization_barrier(jnp.sum(exp_logits, axis=0))
    pos_sum = jnp.sum(jnp.where(positive_hit, logits, 0.0))
    mean_loss = (jnp.sum(jnp.log(partition)) - pos_sum) / QUERIES
    factor = exp_logits / partition[None, :] - positive_hit.astype(jnp.float32)

    def passage_grads(items):
        block, block_totals, block_factor = items
        weights = passage_weights(block)
        shaped = weights.reshape(PAS_LEN, QUERIES, QLEN) / block_totals.reshape(1, QUERIES, QLEN)
        coeffs = (shaped * (logit_gain * block_factor)[None, :, None]).astype(jnp.bfloat16)
        return jnp.dot(coeffs.reshape(PAS_LEN, QUERIES * QLEN), query_rows, preferred_element_type=jnp.float32)
    grad_unit = lax.map(passage_grads, (unit_vec, totals, factor)).reshape(TOKENS, DIM)
    grad_vec = ((grad_unit - unit_f32 * lax.optimization_barrier(jnp.sum(unit_f32 * grad_unit, axis=1, keepdims=True))) / radius).astype(jnp.bfloat16)
    grad_projection = lax.dot_general(states, grad_vec, (((0,), (0,)), ((), ())), preferred_element_type=jnp.float32)
    return (states, grad_projection, mean_loss)
```

```python
import jax
import jax.numpy as jnp
from jax import lax
from jax.experimental import pallas as pl
from jax.experimental.pallas import tpu as pltpu
from jax.sharding import PartitionSpec as P

PAS_LEN = 180
HEAD = 8

soft_temp = 0.05
logit_gain = 1.5
norm_eps = 1e-06
F32 = jnp.float32
BF16 = jnp.bfloat16


def unit_rows(values):
    values = values.astype(F32)
    radius = jnp.sqrt(jnp.sum(values * values, axis=-1, keepdims=True) + norm_eps)
    return (values / radius, radius)


def hidden_kernel(x_ref, w_ref, h_ref, acc_ref):
    step = pl.program_id(0)
    part = lax.dot_general(
        x_ref[...], w_ref[0], (((1,), (1,)), ((), ())), preferred_element_type=F32
    )

    @pl.when(step == 0)
    def _():
        acc_ref[...] = part

    @pl.when(step > 0)
    def _():
        acc_ref[...] += part

    @pl.when(step == pl.num_programs(0) - 1)
    def _():
        half = acc_ref.shape[1] // 2
        gate = acc_ref[:, :half]
        up = acc_ref[:, half:]
        h_ref[...] = (gate / (1.0 + jnp.exp(-gate)) * up).astype(BF16)


def hidden_rows(rows, gate_up):
    count, model = rows.shape
    reps, wide, width = gate_up.shape
    return pl.pallas_call(
        hidden_kernel,
        grid=(reps,),
        in_specs=[
            pl.BlockSpec((count, width), lambda r: (0, r)),
            pl.BlockSpec((1, wide, width), lambda r: (r, 0, 0)),
        ],
        out_specs=pl.BlockSpec((count, wide // 2), lambda r: (0, 0)),
        out_shape=jax.ShapeDtypeStruct((count, wide // 2), BF16),
        scratch_shapes=[pltpu.VMEM((count, wide), F32)],
        compiler_params=pltpu.CompilerParams(vmem_limit_bytes=40 * 2**20),
        cost_estimate=pl.CostEstimate(
            flops=2 * count * model * wide, bytes_accessed=2 * wide * model, transcendentals=0
        ),
    )(rows, gate_up)


def out_kernel(h_ref, w_ref, o_ref):
    o_ref[...] = jnp.dot(h_ref[...], w_ref[0], preferred_element_type=F32).astype(BF16)


def out_rows(hidden, down):
    count, ff = hidden.shape
    reps, _, width = down.shape
    return pl.pallas_call(
        out_kernel,
        grid=(reps,),
        in_specs=[
            pl.BlockSpec((count, ff), lambda r: (0, 0)),
            pl.BlockSpec((1, ff, width), lambda r: (r, 0, 0)),
        ],
        out_specs=pl.BlockSpec((count, width), lambda r: (0, r)),
        out_shape=jax.ShapeDtypeStruct((count, reps * width), BF16),
        compiler_params=pltpu.CompilerParams(vmem_limit_bytes=40 * 2**20),
        cost_estimate=pl.CostEstimate(
            flops=2 * count * ff * reps * width, bytes_accessed=2 * ff * reps * width, transcendentals=0
        ),
    )(hidden, down)


def body(
    passages_in,
    routes,
    route_weights,
    gate_weight,
    up_weight,
    down_weight,
    projection,
    queries,
    positives,
):
    tok_count, model_width = passages_in.shape
    top_count = routes.shape[1]
    experts = lax.axis_size("exp")
    rep_count = lax.axis_size("rep")
    capacity = max(2, 2 * tok_count * top_count // experts)
    tail = capacity - HEAD
    pieces = model_width // 128

    gate_up = jnp.concatenate([gate_weight[0].T, up_weight[0].T], axis=0)
    gate_up = lax.all_gather(gate_up, "rep", axis=0, tiled=False)
    down = lax.all_gather(down_weight[0], "rep", axis=0, tiled=False)

    flat = routes.T.reshape(-1)
    onehot = flat[:, None] == jnp.arange(experts, dtype=jnp.int32)[None, :]
    count = flat.shape[0]
    before = jnp.arange(count)[:, None] > jnp.arange(count)[None, :]
    earlier = jnp.dot(before.astype(BF16), onehot.astype(BF16), preferred_element_type=F32)
    rank = jnp.sum(jnp.where(onehot, earlier, 0.0), axis=1).astype(jnp.int32)
    head_place = jnp.where(rank < HEAD, flat * HEAD + rank, -1).reshape(top_count, tok_count)
    tail_place = jnp.where(rank >= HEAD, flat * tail + rank - HEAD, -1).reshape(top_count, tok_count)

    def dispatch(place, slots):
        hit = place[:, None, :] == jnp.arange(slots, dtype=jnp.int32)[None, :, None]
        return jnp.dot(
            jnp.any(hit, axis=0).astype(BF16), passages_in, preferred_element_type=F32
        ).astype(BF16)

    def exchange(rows, shape):
        moved = lax.all_to_all(rows.reshape(shape), "exp", split_axis=0, concat_axis=0, tiled=True)
        return moved.reshape(rows.shape)

    head_shape = (experts, HEAD, model_width)
    tail_shape = (experts, tail * pieces, 128)
    head_in = exchange(dispatch(head_place, experts * HEAD), head_shape)
    tail_in = exchange(dispatch(tail_place, experts * tail), tail_shape)
    head_hidden = hidden_rows(head_in, gate_up)
    tail_hidden = hidden_rows(tail_in, gate_up)
    head_back = exchange(out_rows(head_hidden, down), head_shape)
    tail_back = exchange(out_rows(tail_hidden, down), tail_shape)

    def combine(place, back):
        slots = back.shape[0]
        hit = place[:, :, None] == jnp.arange(slots, dtype=jnp.int32)[None, None, :]
        mix = jnp.sum(jnp.where(hit, route_weights.T[:, :, None], 0.0), axis=0)
        high = mix.astype(BF16)
        low = (mix - high.astype(F32)).astype(BF16)
        return jnp.dot(high, back, preferred_element_type=F32) + jnp.dot(
            low, back, preferred_element_type=F32
        )

    states = (
        passages_in.astype(F32) + combine(head_place, head_back) + combine(tail_place, tail_back)
    ).astype(BF16)

    projected = jnp.dot(states, projection, preferred_element_type=F32)
    unit_f32, radius = unit_rows(projected)
    unit_vec = unit_f32.astype(BF16)
    query_unit = unit_rows(queries)[0].astype(BF16)
    query_block, query_len, unit_width = queries.shape
    total_queries = query_block * rep_count
    all_queries = lax.all_gather(query_unit, "rep", axis=0, tiled=True)
    query_rows = all_queries.reshape(total_queries * query_len, unit_width)
    owner = lax.axis_index(("exp", "rep"))

    scores = lax.dot_general(
        unit_vec, query_rows, (((1,), (1,)), ((), ())), preferred_element_type=F32
    )
    weights = jnp.exp(scores / soft_temp)
    totals = jnp.sum(weights, axis=0)
    logits = logit_gain * jnp.sum(
        (soft_temp * jnp.log(totals)).reshape(total_queries, query_len), axis=1
    )
    positive_hit = owner == positives
    exp_logits = jnp.exp(logits)

    def total_over(values, axis):
        size = lax.axis_size(axis)
        sent = jnp.broadcast_to(values[None], (size,) + values.shape)
        return jnp.sum(lax.all_to_all(sent, axis, 0, 0, tiled=True), axis=0)

    shares = jnp.stack([exp_logits, jnp.where(positive_hit, logits, 0.0)])
    sums = total_over(total_over(shares, "exp"), "rep")
    partition = sums[0]
    mean_loss = (jnp.sum(jnp.log(partition)) - jnp.sum(sums[1])) / total_queries
    factor = exp_logits / partition - positive_hit.astype(F32)
    scale = (logit_gain * factor)[:, None] / totals.reshape(total_queries, query_len)
    coeffs = (weights * scale.reshape(1, -1)).astype(BF16)
    grad_unit = jnp.dot(coeffs, query_rows, preferred_element_type=F32)
    grad_vec = (
        (grad_unit - unit_f32 * jnp.sum(unit_f32 * grad_unit, axis=1, keepdims=True)) / radius
    ).astype(BF16)
    share = lax.dot_general(
        states, grad_vec, (((0,), (0,)), ((), ())), preferred_element_type=F32
    ).astype(BF16)
    rows_out = model_width // experts
    parts = lax.all_to_all(
        share.reshape(experts, rows_out, unit_width), "exp", split_axis=0, concat_axis=0, tiled=True
    )
    grad_projection = total_over(jnp.sum(parts.astype(F32), axis=0), "rep")
    return (states, grad_projection, mean_loss)


def solution(mesh):
    in_specs = (
        P(("exp", "rep"), None),
        P(("exp", "rep"), None),
        P(("exp", "rep"), None),
        P("exp", "rep", None),
        P("exp", "rep", None),
        P("exp", None, "rep"),
        P(),
        P("rep", None, None),
        P(),
    )
    out_specs = (P(("exp", "rep"), None), P("exp", None), P())
    return jax.shard_map(body, mesh=mesh, in_specs=in_specs, out_specs=out_specs, check_vma=False)
```

```python
import jax
import jax.numpy as jnp
from jax import lax
from jax.experimental import pallas as pl
from jax.experimental.pallas import tpu as pltpu
from jax.sharding import PartitionSpec as P

HEAD = 8
LANES = 128

soft_temp = 0.05
logit_gain = 1.5
norm_eps = 1e-06
F32 = jnp.float32
BF16 = jnp.bfloat16
NT = (((1,), (1,)), ((), ()))
VMEM = pl.BlockSpec(memory_space=pltpu.VMEM)
HBM = pl.BlockSpec(memory_space=pl.ANY)
SMEM = pl.BlockSpec(memory_space=pltpu.SMEM)
PARAMS = pltpu.CompilerParams(vmem_limit_bytes=56 * 2**20)


def kernel_call(kernel, outs, ins, args, scratch=(), flops=0, moved=0):
    return pl.pallas_call(
        kernel,
        in_specs=ins,
        out_specs=[VMEM] * len(outs),
        out_shape=[jax.ShapeDtypeStruct(*o) for o in outs],
        scratch_shapes=scratch,
        compiler_params=PARAMS,
        cost_estimate=pl.CostEstimate(flops=flops, bytes_accessed=moved, transcendentals=0),
    )(*args)


def lane_block(c):
    return slice(c * LANES, (c + 1) * LANES)


def put_head(out_ref, c, values):
    out_ref[:, c, :, :] = values.reshape(-1, HEAD, LANES).astype(BF16)


def get_head(in_ref, c):
    return in_ref[:, c, :, :].astype(F32).reshape(-1, LANES).astype(BF16)


def put_tail(fold_ref, c, values):
    rows = values.shape[0]
    fold_ref[pl.ds((c // 8) * rows * 8 + c % 8, rows, stride=8), :] = values


def get_tail(fold_ref, c, rows):
    return fold_ref[pl.ds((c // 8) * rows * 8 + c % 8, rows, stride=8), :].astype(BF16)


def store_tail(out_ref, fold_ref, blocks, tail):
    experts = out_ref.shape[0]
    span = experts * tail * 8
    for group in range(blocks // 8):
        first = blocks + group * tail
        out_ref[:, first : first + tail, :, :] = (
            fold_ref[group * span : (group + 1) * span, :].reshape(experts, tail, 8, LANES).astype(BF16)
        )


def load_tail(in_ref, fold_ref, blocks, tail):
    experts = in_ref.shape[0]
    span = experts * tail * 8
    for group in range(blocks // 8):
        first = blocks + group * tail
        fold_ref[group * span : (group + 1) * span, :] = (
            in_ref[:, first : first + tail, :, :].astype(F32).reshape(span, LANES)
        )


def pack_kernel(tail, routes_ref, x_ref, out_ref, fold_ref):
    experts = out_ref.shape[0]
    tokens, width = x_ref.shape
    blocks = width // LANES
    routes = routes_ref[...]
    expert_id = lax.broadcasted_iota(jnp.int32, (experts, tokens), 0)
    earlier = lax.broadcasted_iota(jnp.int32, (tokens, tokens), 0) < lax.broadcasted_iota(
        jnp.int32, (tokens, tokens), 1
    )
    earlier = earlier.astype(F32).astype(BF16)
    seen = jnp.zeros((experts, 1), F32)
    picks = []
    for k in range(routes.shape[0]):
        route = routes[k : k + 1, :]
        hit = (expert_id == route).astype(F32)
        ahead = jnp.dot(hit.astype(BF16), earlier, preferred_element_type=F32) + seen
        rank = jnp.sum(hit * ahead, axis=0, keepdims=True).astype(jnp.int32)
        seen = seen + jnp.sum(hit, axis=1, keepdims=True)
        picks.append((route, rank))
    head_row = lax.broadcasted_iota(jnp.int32, (experts * HEAD, tokens), 0)
    tail_row = lax.broadcasted_iota(jnp.int32, (experts * tail, tokens), 0)
    head_pick = jnp.zeros(head_row.shape, F32)
    tail_pick = jnp.zeros(tail_row.shape, F32)
    for route, rank in picks:
        head_place = jnp.where(rank < HEAD, route * HEAD + rank, -1)
        tail_place = jnp.where(rank >= HEAD, route * tail + rank - HEAD, -1)
        head_pick = head_pick + (head_row == head_place).astype(F32)
        tail_pick = tail_pick + (tail_row == tail_place).astype(F32)
    head_pick = head_pick.astype(BF16)
    tail_pick = tail_pick.astype(BF16)
    for c in range(0, blocks, 2):
        columns = x_ref[:, c * LANES : (c + 2) * LANES]
        rows = jnp.dot(head_pick, columns, preferred_element_type=F32)
        put_head(out_ref, c, rows[:, :LANES])
        put_head(out_ref, c + 1, rows[:, LANES:])
        rows = jnp.dot(tail_pick, columns, preferred_element_type=F32)
        put_tail(fold_ref, c, rows[:, :LANES])
        put_tail(fold_ref, c + 1, rows[:, LANES:])
    store_tail(out_ref, fold_ref, blocks, tail)


def pack(routes_t, x, experts, tail):
    blocks = x.shape[1] // LANES
    tiles = blocks + blocks // 8 * tail
    (out,) = kernel_call(
        lambda *refs: pack_kernel(tail, *refs),
        [((experts, tiles, 8, LANES), BF16)],
        [VMEM, VMEM],
        (routes_t, x),
        [pltpu.VMEM((blocks * experts * tail, LANES), F32)],
    )
    return out


def down_half(tail, hidden, wd_ref, out_ref, fold_ref):
    experts = out_ref.shape[0]
    pairs = wd_ref.shape[0]
    for p in range(pairs):
        rows = jnp.dot(hidden, wd_ref[p], preferred_element_type=F32)
        for j in range(2):
            c = 2 * p + j
            put_head(out_ref, c, rows[: experts * HEAD, lane_block(j)])
            put_tail(fold_ref, c, rows[experts * HEAD :, lane_block(j)])
    store_tail(out_ref, fold_ref, 2 * pairs, tail)


def down_copies(w_ref, base, wd_ref, sems):
    reps = w_ref.shape[0]
    half = wd_ref.shape[1] // 2
    return [
        pltpu.make_async_copy(
            w_ref.at[r, pl.ds(base, half), pl.ds(j * LANES, LANES)],
            wd_ref.at[r // 2, pl.ds(j * half, half), pl.ds((r % 2) * LANES, LANES)],
            sems.at[2 * r + j],
        )
        for r in range(reps)
        for j in range(2)
    ]


def expert_kernel(tail, in_ref, w_ref, hid_ref, out_ref, rows_ref, wv_ref, wd_ref, fold_ref, back_ref, sems, down_sems):
    reps, wide, depth = wv_ref.shape
    ff = wide // 2
    experts = in_ref.shape[0]
    blocks = rows_ref.shape[1] // LANES
    first = experts * HEAD
    count = rows_ref.shape[0]
    copies = [
        pltpu.make_async_copy(w_ref.at[r, pl.ds(0, wide)], wv_ref.at[r], sems.at[r]) for r in range(reps)
    ]
    downs = down_copies(w_ref, wide, wd_ref, down_sems)
    for copy in copies + downs:
        copy.start()
    load_tail(in_ref, fold_ref, blocks, tail)
    for c in range(blocks):
        rows_ref[:first, lane_block(c)] = get_head(in_ref, c)
        rows_ref[first:, lane_block(c)] = get_tail(fold_ref, c, count - first)
    step = count // 2
    for i in range(2):
        part = slice(i * step, (i + 1) * step)
        gate = up = None
        for r in range(reps):
            if i == 0:
                copies[r].wait()
            rows = rows_ref[part, r * depth : (r + 1) * depth]
            g = lax.dot_general(rows, wv_ref[r, :ff, :], NT, preferred_element_type=F32)
            u = lax.dot_general(rows, wv_ref[r, ff:, :], NT, preferred_element_type=F32)
            gate = g if gate is None else gate + g
            up = u if up is None else up + u
        hid_ref[part, :] = (gate / (1.0 + jnp.exp(-gate)) * up).astype(BF16)
    for copy in downs:
        copy.wait()
    down_half(tail, hid_ref[...], wd_ref, out_ref, back_ref)


def second_kernel(tail, hid_ref, w_ref, out_ref, wd_ref, back_ref, down_sems):
    downs = down_copies(w_ref, 0, wd_ref, down_sems)
    for copy in downs:
        copy.start()
    for copy in downs:
        copy.wait()
    down_half(tail, hid_ref[...], wd_ref, out_ref, back_ref)


def mix_half(half, back_ref, high_ref, low_ref, x_ref, proj_ref, fold_ref, tail, store):
    experts = back_ref.shape[0]
    blocks = x_ref.shape[1] // (2 * LANES)
    first = experts * HEAD
    load_tail(back_ref, fold_ref, blocks, tail)
    projected = None
    for p in range(blocks // 2):
        cs = (2 * p, 2 * p + 1)
        head = jnp.concatenate([get_head(back_ref, c) for c in cs], axis=1)
        rest = jnp.concatenate([get_tail(fold_ref, c, experts * tail) for c in cs], axis=1)
        added = (
            jnp.dot(high_ref[:, :first], head, preferred_element_type=F32)
            + jnp.dot(low_ref[:, :first], head, preferred_element_type=F32)
            + jnp.dot(high_ref[:, first:], rest, preferred_element_type=F32)
            + jnp.dot(low_ref[:, first:], rest, preferred_element_type=F32)
        )
        states = []
        projs = []
        for j, c in enumerate(cs):
            columns = lane_block(2 * c + half)
            value = (x_ref[:, columns].astype(F32) + added[:, lane_block(j)]).astype(BF16)
            store(c, value)
            states.append(value)
            projs.append(proj_ref[columns, :])
        part = jnp.dot(
            jnp.concatenate(states, axis=1), jnp.concatenate(projs, axis=0), preferred_element_type=F32
        )
        projected = part if projected is None else projected + part
    return projected


def mix_kernel(tail, back_ref, high_ref, low_ref, x_ref, proj_ref, half_ref, sum_ref, fold_ref):
    def store(c, value):
        half_ref[:, lane_block(c)] = value

    sum_ref[...] = mix_half(0, back_ref, high_ref, low_ref, x_ref, proj_ref, fold_ref, tail, store)


def score_kernel(
    tail, gain, owner_ref, back_ref, high_ref, low_ref, x_ref, proj_ref, half_ref, sum_ref, query_ref, positive_ref,
    states_ref, weights_ref, unit_ref, radius_ref, totals_ref, logits_ref, shares_ref, fold_ref,
):
    def store(c, value):
        states_ref[:, lane_block(2 * c)] = half_ref[:, lane_block(c)]
        states_ref[:, lane_block(2 * c + 1)] = value

    projected = sum_ref[...] + mix_half(
        1, back_ref, high_ref, low_ref, x_ref, proj_ref, fold_ref, tail, store
    )
    radius = jnp.sqrt(jnp.sum(projected * projected, axis=1, keepdims=True) + norm_eps)
    unit = projected / radius
    unit_ref[...] = unit
    radius_ref[...] = jnp.broadcast_to(radius, radius_ref.shape)
    unit_vec = unit.astype(BF16)
    step = 4 * LANES
    logits = jnp.zeros((1, LANES), F32)
    for n in range(0, query_ref.shape[0], step):
        scores = lax.dot_general(unit_vec, query_ref[n : n + step, :], NT, preferred_element_type=F32)
        weights = jnp.exp(scores / soft_temp)
        weights_ref[:, n : n + step] = weights
        totals = jnp.sum(weights, axis=0, keepdims=True)
        totals_ref[:, n : n + step] = totals
        logs = soft_temp * jnp.log(totals)
        for j in range(step // LANES):
            logits = logits + logs[:, lane_block(j)]
    logits = gain * logits
    logits_ref[...] = logits
    held = jnp.where(positive_ref[...] == owner_ref[0, 0], logits, 0.0)
    odd = lax.broadcasted_iota(jnp.int32, shares_ref.shape, 0) % 2
    shares_ref[...] = jnp.where(odd == 0, jnp.exp(logits), held)


def grad_kernel(
    gain, owner_ref, sums_ref, logits_ref, positive_ref, weights_ref, totals_ref, query_ref, unit_ref, radius_ref,
    states_ref, share_ref, loss_ref,
):
    senders = sums_ref.shape[0] // 2
    partition = jnp.sum(sums_ref[pl.ds(0, senders, stride=2), :], axis=0, keepdims=True)
    held = jnp.sum(sums_ref[pl.ds(1, senders, stride=2), :], axis=0, keepdims=True)
    loss = jnp.sum(jnp.log(partition) - held, axis=1, keepdims=True) / partition.shape[1]
    loss_ref[...] = jnp.broadcast_to(loss, loss_ref.shape)
    positive = (positive_ref[...] == owner_ref[0, 0]).astype(F32)
    factor = gain * (jnp.exp(logits_ref[...]) / partition - positive)
    step = 4 * LANES
    grad = None
    for n in range(0, query_ref.shape[0], step):
        scale = jnp.concatenate([factor] * (step // LANES), axis=1) / totals_ref[:, n : n + step]
        coeffs = (weights_ref[:, n : n + step] * scale).astype(BF16)
        part = jnp.dot(coeffs, query_ref[n : n + step, :], preferred_element_type=F32)
        grad = part if grad is None else grad + part
    unit = unit_ref[...]
    along = jnp.sum(unit * grad, axis=1, keepdims=True)
    grad_vec = ((grad - unit * along) / radius_ref[...]).astype(BF16)
    share_ref[...] = lax.dot_general(
        states_ref[...], grad_vec, (((0,), (0,)), ((), ())), preferred_element_type=F32
    ).astype(BF16)


def body(
    passages_in,
    routes,
    route_weights,
    gate_weight,
    up_weight,
    down_weight,
    projection,
    queries,
    positives,
):
    tok_count, model_width = passages_in.shape
    top_count = routes.shape[1]
    experts = lax.axis_size("exp")
    rep_count = lax.axis_size("rep")
    ff = gate_weight.shape[2]
    capacity = max(2, 2 * tok_count * top_count // experts)
    tail = capacity - HEAD
    slots = experts * capacity
    blocks = model_width // LANES
    fold = experts * tail * 8

    down = down_weight[0]
    down_halves = [
        jnp.concatenate([down[: ff // 2, lane_block(h)], down[ff // 2 :, lane_block(h)]], axis=1) for h in range(2)
    ]
    first_part = jnp.concatenate([gate_weight[0].T, up_weight[0].T, down_halves[0]], axis=0)
    first_all = lax.all_gather(first_part, "rep", axis=0, tiled=False)
    second_all = lax.all_gather(down_halves[1], "rep", axis=0, tiled=False)

    def exchange(tiles):
        return lax.all_to_all(tiles, "exp", split_axis=0, concat_axis=0, tiled=True)

    packed = pack(routes.T, passages_in, experts, tail)
    arrived = exchange(packed)

    half_tiles = ((experts, blocks // 2 + blocks // 16 * tail, 8, LANES), BF16)
    hidden, send_a = kernel_call(
        lambda *refs: expert_kernel(tail, *refs),
        [((slots, ff), BF16), half_tiles],
        [VMEM, HBM],
        (arrived, first_all),
        [
            pltpu.VMEM((slots, model_width), BF16),
            pltpu.VMEM((rep_count, 2 * ff, model_width // rep_count), BF16),
            pltpu.VMEM((rep_count // 2, ff, 2 * LANES), BF16),
            pltpu.VMEM((2 * fold, LANES), F32),
            pltpu.VMEM((fold, LANES), F32),
            pltpu.SemaphoreType.DMA((rep_count,)),
            pltpu.SemaphoreType.DMA((2 * rep_count,)),
        ],
    )
    back_a = exchange(send_a)
    (send_b,) = kernel_call(
        lambda *refs: second_kernel(tail, *refs),
        [half_tiles],
        [VMEM, HBM],
        (hidden, second_all),
        [
            pltpu.VMEM((rep_count // 2, ff, 2 * LANES), BF16),
            pltpu.VMEM((fold, LANES), F32),
            pltpu.SemaphoreType.DMA((2 * rep_count,)),
        ],
    )
    back_b = exchange(send_b)

    later_routes, _ = lax.optimization_barrier((routes, packed))
    flat = later_routes.T.reshape(-1)
    count = flat.shape[0]
    onehot = flat[:, None] == jnp.arange(experts, dtype=jnp.int32)[None, :]
    before = jnp.arange(count)[:, None] > jnp.arange(count)[None, :]
    earlier = jnp.dot(before.astype(BF16), onehot.astype(BF16), preferred_element_type=F32)
    rank = jnp.sum(jnp.where(onehot, earlier, 0.0), axis=1).astype(jnp.int32)
    place = jnp.where(rank < HEAD, flat * HEAD + rank, experts * HEAD + flat * tail + rank - HEAD)
    place = place.reshape(top_count, tok_count)
    hit = place[:, :, None] == jnp.arange(slots, dtype=jnp.int32)[None, None, :]
    mix = jnp.sum(jnp.where(hit, route_weights.T[:, :, None], 0.0), axis=0)
    high = mix.astype(BF16)
    low = (mix - high.astype(F32)).astype(BF16)

    wide_queries = queries.astype(F32)
    query_radius = jnp.sqrt(jnp.sum(wide_queries * wide_queries, axis=-1, keepdims=True) + norm_eps)
    query_unit = (wide_queries / query_radius).astype(BF16)
    query_block, query_len, unit_width = queries.shape
    total_queries = query_block * rep_count
    all_queries = lax.all_gather(query_unit.transpose(1, 0, 2), "rep", axis=0, tiled=False)
    query_rows = all_queries.transpose(1, 0, 2, 3).reshape(query_len * total_queries, unit_width)

    owner = lax.axis_index(("exp", "rep")).astype(jnp.int32).reshape(1, 1)
    positive_row = positives.reshape(1, total_queries)

    states_a, sum_a = kernel_call(
        lambda *refs: mix_kernel(tail, *refs),
        [((tok_count, model_width // 2), BF16), ((tok_count, unit_width), F32)],
        [VMEM] * 5,
        (back_a, high, low, passages_in, projection),
        [pltpu.VMEM((fold, LANES), F32)],
    )
    devices = experts * rep_count
    columns = query_len * total_queries
    states, weights, unit, radius, totals, logits, shares = kernel_call(
        lambda *refs: score_kernel(tail, logit_gain, *refs),
        [
            ((tok_count, model_width), BF16),
            ((tok_count, columns), F32),
            ((tok_count, unit_width), F32),
            ((tok_count, unit_width), F32),
            ((1, columns), F32),
            ((1, total_queries), F32),
            ((2 * devices, total_queries), F32),
        ],
        [SMEM] + [VMEM] * 9,
        (owner, back_b, high, low, passages_in, projection, states_a, sum_a, query_rows, positive_row),
        [pltpu.VMEM((fold, LANES), F32)],
    )
    sums = lax.all_to_all(
        shares.reshape(devices, 2, total_queries), ("exp", "rep"), split_axis=0, concat_axis=0, tiled=True
    ).reshape(2 * devices, total_queries)
    share, loss = kernel_call(
        lambda *refs: grad_kernel(logit_gain, *refs),
        [((model_width, unit_width), BF16), ((1, LANES), F32)],
        [SMEM] + [VMEM] * 9,
        (owner, sums, logits, positive_row, weights, totals, query_rows, unit, radius, states),
    )
    rows_out = model_width // experts
    parts = exchange(share.reshape(experts, rows_out, unit_width))
    part_sum = jnp.sum(parts.astype(F32), axis=0)
    sent = jnp.broadcast_to(part_sum[None], (rep_count,) + part_sum.shape)
    grad_projection = jnp.sum(lax.all_to_all(sent, "rep", split_axis=0, concat_axis=0, tiled=True), axis=0)
    return (states, grad_projection, loss[0, 0])


def solution(mesh):
    in_specs = (
        P(("exp", "rep"), None),
        P(("exp", "rep"), None),
        P(("exp", "rep"), None),
        P("exp", "rep", None),
        P("exp", "rep", None),
        P("exp", None, "rep"),
        P(),
        P("rep", None, None),
        P(),
    )
    out_specs = (P(("exp", "rep"), None), P("exp", None), P())
    return jax.shard_map(body, mesh=mesh, in_specs=in_specs, out_specs=out_specs, check_vma=False)
```

```python
import jax
import jax.numpy as jnp
from jax import lax
from jax.experimental import pallas as pl
from jax.experimental.pallas import tpu as pltpu
from jax.sharding import PartitionSpec as P

HEAD = 8
LANES = 128

soft_temp = 0.05
logit_gain = 1.5
norm_eps = 1e-06
F32 = jnp.float32
BF16 = jnp.bfloat16
NT = (((1,), (1,)), ((), ()))
VMEM = pl.BlockSpec(memory_space=pltpu.VMEM)
HBM = pl.BlockSpec(memory_space=pl.ANY)
SMEM = pl.BlockSpec(memory_space=pltpu.SMEM)
PARAMS = pltpu.CompilerParams(vmem_limit_bytes=56 * 2**20)


def kernel_call(kernel, outs, ins, args, scratch=(), room=24):
    return pl.pallas_call(
        kernel,
        in_specs=ins,
        out_specs=[VMEM] * len(outs),
        out_shape=[jax.ShapeDtypeStruct(*o) for o in outs],
        scratch_shapes=scratch,
        compiler_params=pltpu.CompilerParams(vmem_limit_bytes=room * 2**20),
    )(*args)


def lane_block(c):
    return slice(c * LANES, (c + 1) * LANES)


def put_head(out_ref, c, values):
    out_ref[:, c, :, :] = values.reshape(-1, HEAD, LANES).astype(BF16)


def get_head(in_ref, c):
    return in_ref[:, c, :, :].astype(F32).reshape(-1, LANES).astype(BF16)


def put_tail(fold_ref, c, values):
    rows = values.shape[0]
    fold_ref[pl.ds((c // 8) * rows * 8 + c % 8, rows, stride=8), :] = values


def get_tail(fold_ref, c, rows):
    return fold_ref[pl.ds((c // 8) * rows * 8 + c % 8, rows, stride=8), :].astype(BF16)


def store_tail(out_ref, fold_ref, blocks, tail):
    experts = out_ref.shape[0]
    span = experts * tail * 8
    for group in range(blocks // 8):
        first = blocks + group * tail
        out_ref[:, first : first + tail, :, :] = (
            fold_ref[group * span : (group + 1) * span, :].reshape(experts, tail, 8, LANES).astype(BF16)
        )


def load_tail(in_ref, fold_ref, blocks, tail):
    experts = in_ref.shape[0]
    span = experts * tail * 8
    for group in range(blocks // 8):
        first = blocks + group * tail
        fold_ref[group * span : (group + 1) * span, :] = (
            in_ref[:, first : first + tail, :, :].astype(F32).reshape(span, LANES)
        )


def pack_kernel(tail, routes_ref, x_ref, out_ref, fold_ref):
    experts = out_ref.shape[0]
    tokens, width = x_ref.shape
    blocks = width // LANES
    routes = routes_ref[...]
    expert_id = lax.broadcasted_iota(jnp.int32, (experts, tokens), 0)
    earlier = lax.broadcasted_iota(jnp.int32, (tokens, tokens), 0) < lax.broadcasted_iota(
        jnp.int32, (tokens, tokens), 1
    )
    earlier = earlier.astype(F32).astype(BF16)
    seen = jnp.zeros((experts, 1), F32)
    picks = []
    for k in range(routes.shape[0]):
        route = routes[k : k + 1, :]
        hit = (expert_id == route).astype(F32)
        ahead = jnp.dot(hit.astype(BF16), earlier, preferred_element_type=F32) + seen
        rank = jnp.sum(hit * ahead, axis=0, keepdims=True).astype(jnp.int32)
        seen = seen + jnp.sum(hit, axis=1, keepdims=True)
        picks.append((route, rank))
    head_row = lax.broadcasted_iota(jnp.int32, (experts * HEAD, tokens), 0)
    tail_row = lax.broadcasted_iota(jnp.int32, (experts * tail, tokens), 0)
    head_pick = jnp.zeros(head_row.shape, F32)
    tail_pick = jnp.zeros(tail_row.shape, F32)
    for route, rank in picks:
        head_place = jnp.where(rank < HEAD, route * HEAD + rank, -1)
        tail_place = jnp.where(rank >= HEAD, route * tail + rank - HEAD, -1)
        head_pick = head_pick + (head_row == head_place).astype(F32)
        tail_pick = tail_pick + (tail_row == tail_place).astype(F32)
    head_pick = head_pick.astype(BF16)
    tail_pick = tail_pick.astype(BF16)
    for c in range(0, blocks, 2):
        columns = x_ref[:, c * LANES : (c + 2) * LANES]
        rows = jnp.dot(head_pick, columns, preferred_element_type=F32)
        put_head(out_ref, c, rows[:, :LANES])
        put_head(out_ref, c + 1, rows[:, LANES:])
        rows = jnp.dot(tail_pick, columns, preferred_element_type=F32)
        put_tail(fold_ref, c, rows[:, :LANES])
        put_tail(fold_ref, c + 1, rows[:, LANES:])
    store_tail(out_ref, fold_ref, blocks, tail)


def pack(routes_t, x, experts, tail):
    blocks = x.shape[1] // LANES
    tiles = blocks + blocks // 8 * tail
    (out,) = kernel_call(
        lambda *refs: pack_kernel(tail, *refs),
        [((experts, tiles, 8, LANES), BF16)],
        [VMEM, VMEM],
        (routes_t, x),
        [pltpu.VMEM((blocks * experts * tail, LANES), F32)],
    )
    return out


def down_half(tail, hidden, wd_ref, out_ref, fold_ref):
    experts = out_ref.shape[0]
    pairs = wd_ref.shape[0]
    for p in range(pairs):
        rows = jnp.dot(hidden, wd_ref[p], preferred_element_type=F32)
        for j in range(2):
            c = 2 * p + j
            put_head(out_ref, c, rows[: experts * HEAD, lane_block(j)])
            put_tail(fold_ref, c, rows[experts * HEAD :, lane_block(j)])
    store_tail(out_ref, fold_ref, 2 * pairs, tail)


def down_copies(w_ref, base, wd_ref, sems):
    reps = w_ref.shape[0]
    half = wd_ref.shape[1] // 2
    return [
        pltpu.make_async_copy(
            w_ref.at[r, pl.ds(base, half), pl.ds(j * LANES, LANES)],
            wd_ref.at[r // 2, pl.ds(j * half, half), pl.ds((r % 2) * LANES, LANES)],
            sems.at[2 * r + j],
        )
        for r in range(reps)
        for j in range(2)
    ]


def expert_kernel(tail, in_ref, w_ref, hid_ref, out_ref, rows_ref, wv_ref, wd_ref, fold_ref, back_ref, sems, down_sems):
    reps, wide, depth = wv_ref.shape
    ff = wide // 2
    experts = in_ref.shape[0]
    blocks = rows_ref.shape[1] // LANES
    first = experts * HEAD
    count = rows_ref.shape[0]
    copies = [
        pltpu.make_async_copy(w_ref.at[r, pl.ds(0, wide)], wv_ref.at[r], sems.at[r]) for r in range(reps)
    ]
    downs = down_copies(w_ref, wide, wd_ref, down_sems)
    for copy in copies + downs:
        copy.start()
    load_tail(in_ref, fold_ref, blocks, tail)
    for c in range(blocks):
        rows_ref[:first, lane_block(c)] = get_head(in_ref, c)
        rows_ref[first:, lane_block(c)] = get_tail(fold_ref, c, count - first)
    step = count // 2
    for i in range(2):
        part = slice(i * step, (i + 1) * step)
        gate = up = None
        for r in range(reps):
            if i == 0:
                copies[r].wait()
            rows = rows_ref[part, r * depth : (r + 1) * depth]
            g = lax.dot_general(rows, wv_ref[r, :ff, :], NT, preferred_element_type=F32)
            u = lax.dot_general(rows, wv_ref[r, ff:, :], NT, preferred_element_type=F32)
            gate = g if gate is None else gate + g
            up = u if up is None else up + u
        hid_ref[part, :] = (gate / (1.0 + jnp.exp(-gate)) * up).astype(BF16)
    for copy in downs:
        copy.wait()
    down_half(tail, hid_ref[...], wd_ref, out_ref, back_ref)


def second_kernel(tail, hid_ref, w_ref, out_ref, wd_ref, back_ref, down_sems):
    downs = down_copies(w_ref, 0, wd_ref, down_sems)
    for copy in downs:
        copy.start()
    for copy in downs:
        copy.wait()
    down_half(tail, hid_ref[...], wd_ref, out_ref, back_ref)


def mix_half(half, back_ref, high_ref, low_ref, x_ref, proj_ref, fold_ref, tail, store):
    experts = back_ref.shape[0]
    blocks = x_ref.shape[1] // (2 * LANES)
    first = experts * HEAD
    load_tail(back_ref, fold_ref, blocks, tail)
    projected = None
    for p in range(blocks // 2):
        cs = (2 * p, 2 * p + 1)
        head = jnp.concatenate([get_head(back_ref, c) for c in cs], axis=1)
        rest = jnp.concatenate([get_tail(fold_ref, c, experts * tail) for c in cs], axis=1)
        added = (
            jnp.dot(high_ref[:, :first], head, preferred_element_type=F32)
            + jnp.dot(low_ref[:, :first], head, preferred_element_type=F32)
            + jnp.dot(high_ref[:, first:], rest, preferred_element_type=F32)
            + jnp.dot(low_ref[:, first:], rest, preferred_element_type=F32)
        )
        states = []
        projs = []
        for j, c in enumerate(cs):
            columns = lane_block(2 * c + half)
            value = (x_ref[:, columns].astype(F32) + added[:, lane_block(j)]).astype(BF16)
            store(c, value)
            states.append(value)
            projs.append(proj_ref[columns, :])
        part = jnp.dot(
            jnp.concatenate(states, axis=1), jnp.concatenate(projs, axis=0), preferred_element_type=F32
        )
        projected = part if projected is None else projected + part
    return projected


def mix_kernel(tail, back_ref, high_ref, low_ref, x_ref, proj_ref, half_ref, sum_ref, fold_ref):
    def store(c, value):
        half_ref[:, lane_block(c)] = value

    sum_ref[...] = mix_half(0, back_ref, high_ref, low_ref, x_ref, proj_ref, fold_ref, tail, store)


def score_kernel(
    tail, gain, owner_ref, back_ref, high_ref, low_ref, x_ref, proj_ref, half_ref, sum_ref, query_ref, positive_ref,
    states_ref, weights_ref, unit_ref, radius_ref, totals_ref, logits_ref, shares_ref, fold_ref,
):
    def store(c, value):
        states_ref[:, lane_block(2 * c)] = half_ref[:, lane_block(c)]
        states_ref[:, lane_block(2 * c + 1)] = value

    projected = sum_ref[...] + mix_half(
        1, back_ref, high_ref, low_ref, x_ref, proj_ref, fold_ref, tail, store
    )
    radius = jnp.sqrt(jnp.sum(projected * projected, axis=1, keepdims=True) + norm_eps)
    unit = projected / radius
    unit_ref[...] = unit
    radius_ref[...] = jnp.broadcast_to(radius, radius_ref.shape)
    unit_vec = unit.astype(BF16)
    step = 4 * LANES
    logits = jnp.zeros((1, LANES), F32)
    for n in range(0, query_ref.shape[0], step):
        scores = lax.dot_general(unit_vec, query_ref[n : n + step, :], NT, preferred_element_type=F32)
        weights = jnp.exp(scores * (1.0 / soft_temp))
        weights_ref[:, n : n + step] = weights
        totals = jnp.sum(weights, axis=0, keepdims=True)
        totals_ref[:, n : n + step] = totals
        logs = soft_temp * jnp.log(totals)
        for j in range(step // LANES):
            logits = logits + logs[:, lane_block(j)]
    logits = gain * logits
    logits_ref[...] = logits
    held = jnp.where(positive_ref[...] == owner_ref[0, 0], logits, 0.0)
    odd = lax.broadcasted_iota(jnp.int32, shares_ref.shape, 0) % 2
    shares_ref[...] = jnp.where(odd == 0, jnp.exp(logits), held)


def grad_kernel(
    gain, owner_ref, sums_ref, logits_ref, positive_ref, weights_ref, totals_ref, query_ref, unit_ref, radius_ref,
    states_ref, share_ref, loss_ref,
):
    senders = sums_ref.shape[0] // 2
    partition = jnp.sum(sums_ref[pl.ds(0, senders, stride=2), :], axis=0, keepdims=True)
    held = jnp.sum(sums_ref[pl.ds(1, senders, stride=2), :], axis=0, keepdims=True)
    loss = jnp.sum(jnp.log(partition) - held, axis=1, keepdims=True) / partition.shape[1]
    loss_ref[...] = jnp.broadcast_to(loss, loss_ref.shape)
    positive = (positive_ref[...] == owner_ref[0, 0]).astype(F32)
    factor = gain * (jnp.exp(logits_ref[...]) / partition - positive)
    step = 4 * LANES
    grad = None
    for n in range(0, query_ref.shape[0], step):
        scale = jnp.concatenate([factor] * (step // LANES), axis=1) / totals_ref[:, n : n + step]
        coeffs = (weights_ref[:, n : n + step] * scale).astype(BF16)
        part = jnp.dot(coeffs, query_ref[n : n + step, :], preferred_element_type=F32)
        grad = part if grad is None else grad + part
    unit = unit_ref[...]
    along = jnp.sum(unit * grad, axis=1, keepdims=True)
    grad_vec = ((grad - unit * along) / radius_ref[...]).astype(BF16)
    share_ref[...] = lax.dot_general(
        states_ref[...], grad_vec, (((0,), (0,)), ((), ())), preferred_element_type=F32
    ).astype(BF16)


def join_kernel(gate_ref, up_ref, down_ref, out_ref, sems):
    ff = gate_ref.shape[0]
    half = ff // 2
    left = pl.ds(0, LANES)
    copies = [
        pltpu.make_async_copy(gate_ref, out_ref.at[pl.ds(0, ff)], sems.at[0]),
        pltpu.make_async_copy(up_ref, out_ref.at[pl.ds(ff, ff)], sems.at[1]),
        pltpu.make_async_copy(
            down_ref.at[pl.ds(0, half), left], out_ref.at[pl.ds(2 * ff, half), left], sems.at[2]
        ),
        pltpu.make_async_copy(
            down_ref.at[pl.ds(half, half), left], out_ref.at[pl.ds(2 * ff, half), pl.ds(LANES, LANES)], sems.at[3]
        ),
    ]
    for copy in copies:
        copy.start()
    for copy in copies:
        copy.wait()


def fan_kernel(copies, in_ref, out_ref):
    rows = in_ref.shape[0] // 2
    even = jnp.sum(in_ref[pl.ds(0, rows, stride=2), :], axis=0, keepdims=True)
    odd = jnp.sum(in_ref[pl.ds(1, rows, stride=2), :], axis=0, keepdims=True)
    parity = lax.broadcasted_iota(jnp.int32, out_ref.shape, 0) % 2
    out_ref[...] = jnp.where(parity == 0, even, odd)


def body(
    passages_in,
    routes,
    route_weights,
    gate_weight,
    up_weight,
    down_weight,
    projection,
    queries,
    positives,
):
    tok_count, model_width = passages_in.shape
    top_count = routes.shape[1]
    experts = lax.axis_size("exp")
    rep_count = lax.axis_size("rep")
    ff = gate_weight.shape[2]
    capacity = max(2, 2 * tok_count * top_count // experts)
    tail = capacity - HEAD
    slots = experts * capacity
    blocks = model_width // LANES
    fold = experts * tail * 8

    down = down_weight[0]
    first_part = pl.pallas_call(
        join_kernel,
        in_specs=[HBM] * 3,
        out_specs=HBM,
        out_shape=jax.ShapeDtypeStruct((5 * ff // 2, 2 * LANES), BF16),
        scratch_shapes=[pltpu.SemaphoreType.DMA((4,))],
        compiler_params=PARAMS,
    )(gate_weight[0].T, up_weight[0].T, down)
    first_all = lax.all_gather(first_part, "rep", axis=0, tiled=False)
    wide_queries = queries.astype(F32)
    query_radius = jnp.sqrt(jnp.sum(wide_queries * wide_queries, axis=-1, keepdims=True) + norm_eps)
    query_unit = (wide_queries / query_radius).astype(BF16)
    query_block, query_len, unit_width = queries.shape
    total_queries = query_block * rep_count
    own_rows = query_unit.transpose(1, 0, 2).reshape(query_len * query_block, unit_width)
    own_half = own_rows.shape[0] // 2
    second_part = jnp.concatenate(
        [
            jnp.concatenate([down[: ff // 2, LANES:], own_rows[:own_half]], axis=0),
            jnp.concatenate([down[ff // 2 :, LANES:], own_rows[own_half:]], axis=0),
        ],
        axis=1,
    )
    second_all = lax.all_gather(second_part, "rep", axis=0, tiled=False)
    query_rows = (
        jnp.concatenate([second_all[:, ff // 2 :, lane_block(h)] for h in range(2)], axis=1)
        .reshape(rep_count, query_len, query_block, unit_width)
        .transpose(1, 0, 2, 3)
        .reshape(query_len * total_queries, unit_width)
    )

    def exchange(tiles):
        return lax.all_to_all(tiles, "exp", split_axis=0, concat_axis=0, tiled=True)

    packed = pack(routes.T, passages_in, experts, tail)
    arrived = exchange(packed)

    half_tiles = ((experts, blocks // 2 + blocks // 16 * tail, 8, LANES), BF16)
    hidden, send_a = kernel_call(
        lambda *refs: expert_kernel(tail, *refs),
        [((slots, ff), BF16), half_tiles],
        [VMEM, HBM],
        (arrived, first_all),
        [
            pltpu.VMEM((slots, model_width), BF16),
            pltpu.VMEM((rep_count, 2 * ff, model_width // rep_count), BF16),
            pltpu.VMEM((rep_count // 2, ff, 2 * LANES), BF16),
            pltpu.VMEM((2 * fold, LANES), F32),
            pltpu.VMEM((fold, LANES), F32),
            pltpu.SemaphoreType.DMA((rep_count,)),
            pltpu.SemaphoreType.DMA((2 * rep_count,)),
        ],
        room=56,
    )
    back_a = exchange(send_a)
    (send_b,) = kernel_call(
        lambda *refs: second_kernel(tail, *refs),
        [half_tiles],
        [VMEM, HBM],
        (hidden, second_all),
        [
            pltpu.VMEM((rep_count // 2, ff, 2 * LANES), BF16),
            pltpu.VMEM((fold, LANES), F32),
            pltpu.SemaphoreType.DMA((2 * rep_count,)),
        ],
        room=56,
    )
    back_b = exchange(send_b)

    later_routes, _ = lax.optimization_barrier((routes, packed))
    flat = later_routes.T.reshape(-1)
    count = flat.shape[0]
    onehot = flat[:, None] == jnp.arange(experts, dtype=jnp.int32)[None, :]
    before = jnp.arange(count)[:, None] > jnp.arange(count)[None, :]
    earlier = jnp.dot(before.astype(BF16), onehot.astype(BF16), preferred_element_type=F32)
    rank = jnp.sum(jnp.where(onehot, earlier, 0.0), axis=1).astype(jnp.int32)
    place = jnp.where(rank < HEAD, flat * HEAD + rank, experts * HEAD + flat * tail + rank - HEAD)
    place = place.reshape(top_count, tok_count)
    hit = place[:, :, None] == jnp.arange(slots, dtype=jnp.int32)[None, None, :]
    mix = jnp.sum(jnp.where(hit, route_weights.T[:, :, None], 0.0), axis=0)
    high = mix.astype(BF16)
    low = (mix - high.astype(F32)).astype(BF16)

    owner = lax.axis_index(("exp", "rep")).astype(jnp.int32).reshape(1, 1)
    positive_row = positives.reshape(1, total_queries)

    states_a, sum_a = kernel_call(
        lambda *refs: mix_kernel(tail, *refs),
        [((tok_count, model_width // 2), BF16), ((tok_count, unit_width), F32)],
        [VMEM] * 5,
        (back_a, high, low, passages_in, projection),
        [pltpu.VMEM((fold, LANES), F32)],
    )
    columns = query_len * total_queries
    states, weights, unit, radius, totals, logits, shares = kernel_call(
        lambda *refs: score_kernel(tail, logit_gain, *refs),
        [
            ((tok_count, model_width), BF16),
            ((tok_count, columns), F32),
            ((tok_count, unit_width), F32),
            ((tok_count, unit_width), F32),
            ((1, columns), F32),
            ((1, total_queries), F32),
            ((2 * experts, total_queries), F32),
        ],
        [SMEM] + [VMEM] * 9,
        (owner, back_b, high, low, passages_in, projection, states_a, sum_a, query_rows, positive_row),
        [pltpu.VMEM((fold, LANES), F32)],
    )
    def share_out(rows, axis):
        pairs = rows.reshape(-1, 2, total_queries)
        return lax.all_to_all(pairs, axis, split_axis=0, concat_axis=0, tiled=True).reshape(rows.shape)

    (fanned,) = kernel_call(
        lambda *refs: fan_kernel(rep_count, *refs),
        [((2 * rep_count, total_queries), F32)],
        [VMEM],
        (share_out(shares, "exp"),),
    )
    sums = share_out(fanned, "rep")
    share, loss = kernel_call(
        lambda *refs: grad_kernel(logit_gain, *refs),
        [((model_width, unit_width), BF16), ((1, LANES), F32)],
        [SMEM] + [VMEM] * 9,
        (owner, sums, logits, positive_row, weights, totals, query_rows, unit, radius, states),
    )
    rows_out = model_width // experts
    parts = exchange(share.reshape(experts, rows_out, unit_width))
    part_sum = jnp.sum(parts.astype(F32), axis=0)
    sent = jnp.broadcast_to(part_sum[None], (rep_count,) + part_sum.shape)
    grad_projection = jnp.sum(lax.all_to_all(sent, "rep", split_axis=0, concat_axis=0, tiled=True), axis=0)
    return (states, grad_projection, loss[0, 0])


def solution(mesh):
    in_specs = (
        P(("exp", "rep"), None),
        P(("exp", "rep"), None),
        P(("exp", "rep"), None),
        P("exp", "rep", None),
        P("exp", "rep", None),
        P("exp", None, "rep"),
        P(),
        P("rep", None, None),
        P(),
    )
    out_specs = (P(("exp", "rep"), None), P("exp", None), P())
    return jax.shard_map(body, mesh=mesh, in_specs=in_specs, out_specs=out_specs, check_vma=False)
```

```python
import jax
import jax.numpy as jnp
from jax import lax
from jax.experimental import pallas as pl
from jax.experimental.pallas import tpu as pltpu
from jax.sharding import PartitionSpec as P

HEAD = 8
LANES = 128

soft_temp = 0.05
logit_gain = 1.5
norm_eps = 1e-06
F32 = jnp.float32
BF16 = jnp.bfloat16
NT = (((1,), (1,)), ((), ()))
VMEM = pl.BlockSpec(memory_space=pltpu.VMEM)
HBM = pl.BlockSpec(memory_space=pl.ANY)
SMEM = pl.BlockSpec(memory_space=pltpu.SMEM)


def kernel_call(kernel, outs, ins, args, scratch=(), room=24, out_specs=None):
    return pl.pallas_call(
        kernel,
        in_specs=ins,
        out_specs=out_specs or [VMEM] * len(outs),
        out_shape=[jax.ShapeDtypeStruct(*o) for o in outs],
        scratch_shapes=scratch,
        compiler_params=pltpu.CompilerParams(vmem_limit_bytes=room * 2**20),
    )(*args)


def lane_block(c):
    return slice(c * LANES, (c + 1) * LANES)


def put_head(out_ref, c, values):
    out_ref[:, c, :, :] = values.reshape(-1, HEAD, LANES).astype(BF16)


def get_head(in_ref, c):
    return in_ref[:, c, :, :].astype(F32).reshape(-1, LANES).astype(BF16)


def put_tail(fold_ref, c, values):
    rows = values.shape[0]
    fold_ref[pl.ds((c // 8) * rows * 8 + c % 8, rows, stride=8), :] = values


def get_tail(fold_ref, c, rows):
    return fold_ref[pl.ds((c // 8) * rows * 8 + c % 8, rows, stride=8), :].astype(BF16)


def store_tail(out_ref, fold_ref, blocks, tail):
    experts = out_ref.shape[0]
    span = experts * tail * 8
    for group in range(blocks // 8):
        first = blocks + group * tail
        out_ref[:, first : first + tail, :, :] = (
            fold_ref[group * span : (group + 1) * span, :].reshape(experts, tail, 8, LANES).astype(BF16)
        )


def load_tail(in_ref, fold_ref, blocks, tail):
    experts = in_ref.shape[0]
    span = experts * tail * 8
    for group in range(blocks // 8):
        first = blocks + group * tail
        fold_ref[group * span : (group + 1) * span, :] = (
            in_ref[:, first : first + tail, :, :].astype(F32).reshape(span, LANES)
        )


def pack_kernel(tail, routes_ref, x_ref, out_ref, fold_ref):
    experts = out_ref.shape[0]
    tokens, width = x_ref.shape
    blocks = width // LANES
    routes = routes_ref[...]
    expert_id = lax.broadcasted_iota(jnp.int32, (experts, tokens), 0)
    earlier = lax.broadcasted_iota(jnp.int32, (tokens, tokens), 0) < lax.broadcasted_iota(
        jnp.int32, (tokens, tokens), 1
    )
    earlier = earlier.astype(F32).astype(BF16)
    seen = jnp.zeros((experts, 1), F32)
    picks = []
    for k in range(routes.shape[0]):
        route = routes[k : k + 1, :]
        hit = (expert_id == route).astype(F32)
        ahead = jnp.dot(hit.astype(BF16), earlier, preferred_element_type=F32) + seen
        rank = jnp.sum(hit * ahead, axis=0, keepdims=True).astype(jnp.int32)
        seen = seen + jnp.sum(hit, axis=1, keepdims=True)
        picks.append((route, rank))
    head_row = lax.broadcasted_iota(jnp.int32, (experts * HEAD, tokens), 0)
    tail_row = lax.broadcasted_iota(jnp.int32, (experts * tail, tokens), 0)
    head_pick = jnp.zeros(head_row.shape, F32)
    tail_pick = jnp.zeros(tail_row.shape, F32)
    for route, rank in picks:
        head_place = jnp.where(rank < HEAD, route * HEAD + rank, -1)
        tail_place = jnp.where(rank >= HEAD, route * tail + rank - HEAD, -1)
        head_pick = head_pick + (head_row == head_place).astype(F32)
        tail_pick = tail_pick + (tail_row == tail_place).astype(F32)
    head_pick = head_pick.astype(BF16)
    tail_pick = tail_pick.astype(BF16)
    for c in range(0, blocks, 2):
        columns = x_ref[:, c * LANES : (c + 2) * LANES]
        rows = jnp.dot(head_pick, columns, preferred_element_type=F32)
        put_head(out_ref, c, rows[:, :LANES])
        put_head(out_ref, c + 1, rows[:, LANES:])
        rows = jnp.dot(tail_pick, columns, preferred_element_type=F32)
        put_tail(fold_ref, c, rows[:, :LANES])
        put_tail(fold_ref, c + 1, rows[:, LANES:])
    store_tail(out_ref, fold_ref, blocks, tail)


def pack(routes_t, x, experts, tail):
    blocks = x.shape[1] // LANES
    tiles = blocks + blocks // 8 * tail
    (out,) = kernel_call(
        lambda *refs: pack_kernel(tail, *refs),
        [((experts, tiles, 8, LANES), BF16)],
        [VMEM, VMEM],
        (routes_t, x),
        [pltpu.VMEM((blocks * experts * tail, LANES), F32)],
    )
    return out


def down_half(tail, hidden, wd_ref, downs, tiles_ref, out_ref, fold_ref, sems):
    experts = tiles_ref.shape[0]
    pairs = wd_ref.shape[0]
    blocks = 2 * pairs
    sent = []

    def send(first, count):
        part = (slice(None), pl.ds(first, count))
        copy = pltpu.make_async_copy(tiles_ref.at[part], out_ref.at[part], sems.at[len(sent)])
        copy.start()
        sent.append(copy)

    for p in range(pairs):
        for copy in downs[4 * p : 4 * p + 4]:
            copy.wait()
        rows = jnp.dot(hidden, wd_ref[p], preferred_element_type=F32)
        for j in range(2):
            put_head(tiles_ref, 2 * p + j, rows[: experts * HEAD, lane_block(j)])
            put_tail(fold_ref, 2 * p + j, rows[experts * HEAD :, lane_block(j)])
        send(2 * p, 2)
    store_tail(tiles_ref, fold_ref, blocks, tail)
    send(blocks, tiles_ref.shape[1] - blocks)
    for copy in sent:
        copy.wait()


def down_copies(w_ref, base, wd_ref, sems):
    reps = w_ref.shape[0]
    half = wd_ref.shape[1] // 2
    return [
        pltpu.make_async_copy(
            w_ref.at[r, pl.ds(base, half), pl.ds(j * LANES, LANES)],
            wd_ref.at[r // 2, pl.ds(j * half, half), pl.ds((r % 2) * LANES, LANES)],
            sems.at[2 * r + j],
        )
        for r in range(reps)
        for j in range(2)
    ]


def unfold_kernel(tail, in_ref, rows_ref, fold_ref):
    blocks = rows_ref.shape[1] // LANES
    first = in_ref.shape[0] * HEAD
    load_tail(in_ref, fold_ref, blocks, tail)
    for c in range(blocks):
        rows_ref[:first, lane_block(c)] = get_head(in_ref, c)
        rows_ref[first:, lane_block(c)] = get_tail(fold_ref, c, rows_ref.shape[0] - first)


def expert_kernel(
    tail, in_ref, w_ref, hid_ref, out_ref, rows_ref, hidden_ref, tiles_ref, wv_ref, wd_ref, fold_ref,
    row_sems, sems, down_sems, hid_sems, send_sems,
):
    reps, wide, depth = wv_ref.shape
    ff = wide // 2
    count = rows_ref.shape[0]
    copies = []
    for r in range(reps):
        columns = pl.ds(r * depth, depth)
        copies.append(
            (
                pltpu.make_async_copy(w_ref.at[r, pl.ds(0, wide)], wv_ref.at[r], sems.at[r]),
                pltpu.make_async_copy(in_ref.at[:, columns], rows_ref.at[:, columns], row_sems.at[r]),
            )
        )
    downs = down_copies(w_ref, wide, wd_ref, down_sems)
    for pair in copies:
        for copy in pair:
            copy.start()
    for copy in downs:
        copy.start()
    step = count // 2
    kept = []
    for i in range(2):
        part = slice(i * step, (i + 1) * step)
        gate = up = None
        for r in range(reps):
            if i == 0:
                for copy in copies[r]:
                    copy.wait()
            rows = rows_ref[part, r * depth : (r + 1) * depth]
            g = lax.dot_general(rows, wv_ref[r, :ff, :], NT, preferred_element_type=F32)
            u = lax.dot_general(rows, wv_ref[r, ff:, :], NT, preferred_element_type=F32)
            gate = g if gate is None else gate + g
            up = u if up is None else up + u
        hidden_ref[part, :] = (gate / (1.0 + jnp.exp(-gate)) * up).astype(BF16)
        span = pl.ds(i * step, step)
        copy = pltpu.make_async_copy(hidden_ref.at[span], hid_ref.at[span], hid_sems.at[i])
        copy.start()
        kept.append(copy)
    down_half(tail, hidden_ref[...], wd_ref, downs, tiles_ref, out_ref, fold_ref, send_sems)
    for copy in kept:
        copy.wait()


def second_kernel(
    tail, hid_ref, w_ref, out_ref, hidden_ref, tiles_ref, wd_ref, fold_ref, hid_sem, down_sems, send_sems
):
    taken = pltpu.make_async_copy(hid_ref, hidden_ref, hid_sem)
    taken.start()
    downs = down_copies(w_ref, 0, wd_ref, down_sems)
    for copy in downs:
        copy.start()
    taken.wait()
    down_half(tail, hidden_ref[...], wd_ref, downs, tiles_ref, out_ref, fold_ref, send_sems)


def mix_half(half, back_ref, high_ref, low_ref, x_ref, proj_ref, fold_ref, tail, store):
    experts = back_ref.shape[0]
    blocks = x_ref.shape[1] // (2 * LANES)
    first = experts * HEAD
    load_tail(back_ref, fold_ref, blocks, tail)
    projected = None
    for p in range(blocks // 2):
        cs = (2 * p, 2 * p + 1)
        head = jnp.concatenate([get_head(back_ref, c) for c in cs], axis=1)
        rest = jnp.concatenate([get_tail(fold_ref, c, experts * tail) for c in cs], axis=1)
        added = (
            jnp.dot(high_ref[:, :first], head, preferred_element_type=F32)
            + jnp.dot(low_ref[:, :first], head, preferred_element_type=F32)
            + jnp.dot(high_ref[:, first:], rest, preferred_element_type=F32)
            + jnp.dot(low_ref[:, first:], rest, preferred_element_type=F32)
        )
        states = []
        projs = []
        for j, c in enumerate(cs):
            columns = lane_block(2 * c + half)
            value = (x_ref[:, columns].astype(F32) + added[:, lane_block(j)]).astype(BF16)
            store(c, value)
            states.append(value)
            projs.append(proj_ref[columns, :])
        part = jnp.dot(
            jnp.concatenate(states, axis=1), jnp.concatenate(projs, axis=0), preferred_element_type=F32
        )
        projected = part if projected is None else projected + part
    return projected


def mix_kernel(tail, back_ref, high_ref, low_ref, x_ref, proj_ref, half_ref, sum_ref, fold_ref):
    def store(c, value):
        half_ref[:, lane_block(c)] = value

    sum_ref[...] = mix_half(0, back_ref, high_ref, low_ref, x_ref, proj_ref, fold_ref, tail, store)


def score_kernel(
    tail, gain, owner_ref, sum_ref, positive_ref, *refs,
):
    far = refs[:7]
    states_out_ref, weights_out_ref, unit_ref, radius_ref, totals_ref, logits_ref, shares_ref = refs[7:14]
    back_ref, high_ref, low_ref, x_ref, proj_ref, half_ref, query_ref = near = refs[14:21]
    fold_ref, states_ref, weights_ref, sems, out_sem, weight_sems = refs[21:]
    loads = [pltpu.make_async_copy(f, n, sems.at[i]) for i, (f, n) in enumerate(zip(far, near))]
    for copy in loads:
        copy.start()
    for copy in loads[:-1]:
        copy.wait()

    def store(c, value):
        states_ref[:, lane_block(2 * c)] = half_ref[:, lane_block(c)]
        states_ref[:, lane_block(2 * c + 1)] = value

    projected = sum_ref[...] + mix_half(
        1, back_ref, high_ref, low_ref, x_ref, proj_ref, fold_ref, tail, store
    )
    copy_out = pltpu.make_async_copy(states_ref, states_out_ref, out_sem)
    copy_out.start()
    loads[-1].wait()
    radius = jnp.sqrt(jnp.sum(projected * projected, axis=1, keepdims=True) + norm_eps)
    unit = projected / radius
    unit_ref[...] = unit
    radius_ref[...] = jnp.broadcast_to(radius, radius_ref.shape)
    unit_vec = unit.astype(BF16)
    step = 4 * LANES
    logits = jnp.zeros((1, LANES), F32)
    kept = [copy_out]
    for n in range(0, query_ref.shape[0], step):
        scores = lax.dot_general(unit_vec, query_ref[n : n + step, :], NT, preferred_element_type=F32)
        weights = jnp.exp(scores * (1.0 / soft_temp))
        weights_ref[:, n : n + step] = weights
        part = (slice(None), pl.ds(n, step))
        copy = pltpu.make_async_copy(weights_ref.at[part], weights_out_ref.at[part], weight_sems.at[n // step])
        copy.start()
        kept.append(copy)
        totals = jnp.sum(weights, axis=0, keepdims=True)
        totals_ref[:, n : n + step] = totals
        logs = soft_temp * jnp.log(totals)
        for j in range(step // LANES):
            logits = logits + logs[:, lane_block(j)]
    logits = gain * logits
    logits_ref[...] = logits
    held = jnp.where(positive_ref[...] == owner_ref[0, 0], logits, 0.0)
    odd = lax.broadcasted_iota(jnp.int32, shares_ref.shape, 0) % 2
    shares_ref[...] = jnp.where(odd == 0, jnp.exp(logits), held)
    for copy in kept:
        copy.wait()


def grad_kernel(
    gain, owner_ref, sums_ref, logits_ref, positive_ref, totals_ref, unit_ref, radius_ref,
    weights_far, query_far, states_far, share_ref, loss_ref, weights_ref, query_ref, states_ref, sems, weight_sems,
):
    step = 4 * LANES
    loads = []
    for i in range(weights_ref.shape[1] // step):
        part = (slice(None), pl.ds(i * step, step))
        loads.append(pltpu.make_async_copy(weights_far.at[part], weights_ref.at[part], weight_sems.at[i]))
    load_query = pltpu.make_async_copy(query_far, query_ref, sems.at[0])
    load_states = pltpu.make_async_copy(states_far, states_ref, sems.at[1])
    for copy in [loads[0], load_query] + loads[1:] + [load_states]:
        copy.start()
    senders = sums_ref.shape[0] // 2
    partition = jnp.sum(sums_ref[pl.ds(0, senders, stride=2), :], axis=0, keepdims=True)
    held = jnp.sum(sums_ref[pl.ds(1, senders, stride=2), :], axis=0, keepdims=True)
    loss = jnp.sum(jnp.log(partition) - held, axis=1, keepdims=True) / partition.shape[1]
    loss_ref[...] = jnp.broadcast_to(loss, loss_ref.shape)
    positive = (positive_ref[...] == owner_ref[0, 0]).astype(F32)
    factor = gain * (jnp.exp(logits_ref[...]) / partition - positive)
    grad = None
    load_query.wait()
    for n in range(0, query_ref.shape[0], step):
        loads[n // step].wait()
        scale = jnp.concatenate([factor] * (step // LANES), axis=1) / totals_ref[:, n : n + step]
        coeffs = (weights_ref[:, n : n + step] * scale).astype(BF16)
        part = jnp.dot(coeffs, query_ref[n : n + step, :], preferred_element_type=F32)
        grad = part if grad is None else grad + part
    unit = unit_ref[...]
    along = jnp.sum(unit * grad, axis=1, keepdims=True)
    grad_vec = ((grad - unit * along) / radius_ref[...]).astype(BF16)
    load_states.wait()
    share_ref[...] = lax.dot_general(
        states_ref[...], grad_vec, (((0,), (0,)), ((), ())), preferred_element_type=F32
    ).astype(BF16)


def join_kernel(gate_ref, up_ref, down_ref, out_ref):
    ff = gate_ref.shape[0]
    half = ff // 2
    out_ref[:ff, :] = gate_ref[...]
    out_ref[ff : 2 * ff, :] = up_ref[...]
    out_ref[2 * ff :, :LANES] = down_ref[:half, :LANES]
    out_ref[2 * ff :, LANES:] = down_ref[half:, :LANES]


def fan_kernel(copies, in_ref, out_ref):
    rows = in_ref.shape[0] // 2
    even = jnp.sum(in_ref[pl.ds(0, rows, stride=2), :], axis=0, keepdims=True)
    odd = jnp.sum(in_ref[pl.ds(1, rows, stride=2), :], axis=0, keepdims=True)
    parity = lax.broadcasted_iota(jnp.int32, out_ref.shape, 0) % 2
    out_ref[...] = jnp.where(parity == 0, even, odd)


def body(
    passages_in,
    routes,
    route_weights,
    gate_weight,
    up_weight,
    down_weight,
    projection,
    queries,
    positives,
):
    tok_count, model_width = passages_in.shape
    top_count = routes.shape[1]
    experts = lax.axis_size("exp")
    rep_count = lax.axis_size("rep")
    ff = gate_weight.shape[2]
    capacity = max(2, 2 * tok_count * top_count // experts)
    tail = capacity - HEAD
    slots = experts * capacity
    blocks = model_width // LANES
    fold = experts * tail * 8

    down = down_weight[0]
    (first_part,) = kernel_call(
        join_kernel,
        [((5 * ff // 2, 2 * LANES), BF16)],
        [VMEM] * 3,
        (gate_weight[0].T, up_weight[0].T, down),
        room=56,
    )
    first_all = lax.all_gather(first_part, "rep", axis=0, tiled=False)
    wide_queries = queries.astype(F32)
    query_radius = jnp.sqrt(jnp.sum(wide_queries * wide_queries, axis=-1, keepdims=True) + norm_eps)
    query_unit = (wide_queries / query_radius).astype(BF16)
    query_block, query_len, unit_width = queries.shape
    total_queries = query_block * rep_count
    own_rows = query_unit.transpose(1, 0, 2).reshape(query_len * query_block, unit_width)
    own_half = own_rows.shape[0] // 2
    second_part = jnp.concatenate(
        [
            jnp.concatenate([down[: ff // 2, LANES:], own_rows[:own_half]], axis=0),
            jnp.concatenate([down[ff // 2 :, LANES:], own_rows[own_half:]], axis=0),
        ],
        axis=1,
    )
    second_all = lax.all_gather(second_part, "rep", axis=0, tiled=False)
    query_rows = (
        jnp.concatenate([second_all[:, ff // 2 :, lane_block(h)] for h in range(2)], axis=1)
        .reshape(rep_count, query_len, query_block, unit_width)
        .transpose(1, 0, 2, 3)
        .reshape(query_len * total_queries, unit_width)
    )

    def exchange(tiles):
        return lax.all_to_all(tiles, "exp", split_axis=0, concat_axis=0, tiled=True)

    packed = pack(routes.T, passages_in, experts, tail)
    arrived = exchange(packed)

    (rows_in,) = kernel_call(
        lambda *refs: unfold_kernel(tail, *refs),
        [((slots, model_width), BF16)],
        [VMEM],
        (arrived,),
        [pltpu.VMEM((2 * fold, LANES), F32)],
        room=56,
    )
    half_tiles = ((experts, blocks // 2 + blocks // 16 * tail, 8, LANES), BF16)
    down_room = [
        pltpu.VMEM((slots, ff), BF16),
        pltpu.VMEM(*half_tiles),
    ]
    pair_room = pltpu.VMEM((rep_count // 2, ff, 2 * LANES), BF16)
    fold_room = pltpu.VMEM((fold, LANES), F32)
    copy_sems = pltpu.SemaphoreType.DMA
    hidden, send_a = kernel_call(
        lambda *refs: expert_kernel(tail, *refs),
        [((slots, ff), BF16), half_tiles],
        [HBM, HBM],
        (rows_in, first_all),
        [pltpu.VMEM((slots, model_width), BF16)]
        + down_room
        + [pltpu.VMEM((rep_count, 2 * ff, model_width // rep_count), BF16), pair_room, fold_room]
        + [copy_sems((rep_count,)), copy_sems((rep_count,)), copy_sems((2 * rep_count,))]
        + [copy_sems((2,)), copy_sems((rep_count // 2 + 1,))],
        room=56,
        out_specs=[HBM, HBM],
    )
    back_a = exchange(send_a)
    (send_b,) = kernel_call(
        lambda *refs: second_kernel(tail, *refs),
        [half_tiles],
        [HBM, HBM],
        (hidden, second_all),
        down_room
        + [pair_room, fold_room, copy_sems, copy_sems((2 * rep_count,)), copy_sems((rep_count // 2 + 1,))],
        room=56,
        out_specs=[HBM],
    )
    back_b = exchange(send_b)

    later_routes, _ = lax.optimization_barrier((routes, packed))
    flat = later_routes.T.reshape(-1)
    count = flat.shape[0]
    onehot = flat[:, None] == jnp.arange(experts, dtype=jnp.int32)[None, :]
    before = jnp.arange(count)[:, None] > jnp.arange(count)[None, :]
    earlier = jnp.dot(before.astype(BF16), onehot.astype(BF16), preferred_element_type=F32)
    rank = jnp.sum(jnp.where(onehot, earlier, 0.0), axis=1).astype(jnp.int32)
    place = jnp.where(rank < HEAD, flat * HEAD + rank, experts * HEAD + flat * tail + rank - HEAD)
    place = place.reshape(top_count, tok_count)
    hit = place[:, :, None] == jnp.arange(slots, dtype=jnp.int32)[None, None, :]
    mix = jnp.sum(jnp.where(hit, route_weights.T[:, :, None], 0.0), axis=0)
    high = mix.astype(BF16)
    low = (mix - high.astype(F32)).astype(BF16)

    owner = lax.axis_index(("exp", "rep")).astype(jnp.int32).reshape(1, 1)
    positive_row = positives.reshape(1, total_queries)

    states_a, sum_a = kernel_call(
        lambda *refs: mix_kernel(tail, *refs),
        [((tok_count, model_width // 2), BF16), ((tok_count, unit_width), F32)],
        [VMEM] * 5,
        (back_a, high, low, passages_in, projection),
        [pltpu.VMEM((fold, LANES), F32)],
    )
    columns = query_len * total_queries
    far = (back_b, high, low, passages_in, projection, states_a, query_rows)
    chunks = columns // (4 * LANES)
    near_weights = pltpu.VMEM((tok_count, columns), F32)
    near_states = pltpu.VMEM((tok_count, model_width), BF16)
    states, weights, unit, radius, totals, logits, shares = kernel_call(
        lambda *refs: score_kernel(tail, logit_gain, *refs),
        [
            ((tok_count, model_width), BF16),
            ((tok_count, columns), F32),
            ((tok_count, unit_width), F32),
            ((tok_count, unit_width), F32),
            ((1, columns), F32),
            ((1, total_queries), F32),
            ((2 * experts, total_queries), F32),
        ],
        [SMEM, VMEM, VMEM] + [HBM] * len(far),
        (owner, sum_a, positive_row) + far,
        [pltpu.VMEM(a.shape, a.dtype) for a in far]
        + [fold_room, near_states, near_weights]
        + [copy_sems((len(far),)), copy_sems, copy_sems((chunks,))],
        room=56,
        out_specs=[HBM] * 2 + [VMEM] * 5,
    )

    def share_out(rows, axis):
        pairs = rows.reshape(-1, 2, total_queries)
        return lax.all_to_all(pairs, axis, split_axis=0, concat_axis=0, tiled=True).reshape(rows.shape)

    (fanned,) = kernel_call(
        lambda *refs: fan_kernel(rep_count, *refs),
        [((2 * rep_count, total_queries), F32)],
        [VMEM],
        (share_out(shares, "exp"),),
    )
    sums = share_out(fanned, "rep")
    share, loss = kernel_call(
        lambda *refs: grad_kernel(logit_gain, *refs),
        [((model_width, unit_width), BF16), ((1, LANES), F32)],
        [SMEM] + [VMEM] * 6 + [HBM] * 3,
        (owner, sums, logits, positive_row, totals, unit, radius, weights, query_rows, states),
        [near_weights, pltpu.VMEM(query_rows.shape, BF16), near_states, copy_sems((2,)), copy_sems((chunks,))],
        room=56,
    )
    rows_out = model_width // experts
    parts = exchange(share.reshape(experts, rows_out, unit_width))
    part_sum = jnp.sum(parts.astype(F32), axis=0)
    sent = jnp.broadcast_to(part_sum[None], (rep_count,) + part_sum.shape)
    grad_projection = jnp.sum(lax.all_to_all(sent, "rep", split_axis=0, concat_axis=0, tiled=True), axis=0)
    return (states, grad_projection, loss[0, 0])


def solution(mesh):
    in_specs = (
        P(("exp", "rep"), None),
        P(("exp", "rep"), None),
        P(("exp", "rep"), None),
        P("exp", "rep", None),
        P("exp", "rep", None),
        P("exp", None, "rep"),
        P(),
        P("rep", None, None),
        P(),
    )
    out_specs = (P(("exp", "rep"), None), P("exp", None), P())
    return jax.shard_map(body, mesh=mesh, in_specs=in_specs, out_specs=out_specs, check_vma=False)
```

```python
import jax
import jax.numpy as jnp
from jax import lax
from jax.experimental import pallas as pl
from jax.experimental.pallas import tpu as pltpu
from jax.sharding import PartitionSpec as P

HEAD = 8
LANES = 128

soft_temp = 0.05
logit_gain = 1.5
norm_eps = 1e-06
F32 = jnp.float32
BF16 = jnp.bfloat16
NT = (((1,), (1,)), ((), ()))
VMEM = pl.BlockSpec(memory_space=pltpu.VMEM)
HBM = pl.BlockSpec(memory_space=pl.ANY)
SMEM = pl.BlockSpec(memory_space=pltpu.SMEM)


def kernel_call(kernel, outs, ins, args, scratch=(), room=24, out_specs=None):
    return pl.pallas_call(
        kernel,
        in_specs=ins,
        out_specs=out_specs or [VMEM] * len(outs),
        out_shape=[jax.ShapeDtypeStruct(*o) for o in outs],
        scratch_shapes=scratch,
        compiler_params=pltpu.CompilerParams(vmem_limit_bytes=room * 2**20),
    )(*args)


def lane_block(c):
    return slice(c * LANES, (c + 1) * LANES)


def put_head(out_ref, c, values):
    out_ref[:, c, :, :] = values.reshape(-1, HEAD, LANES).astype(BF16)


def get_head(in_ref, c):
    return in_ref[:, c, :, :].astype(F32).reshape(-1, LANES).astype(BF16)


def put_tail(fold_ref, c, values):
    rows = values.shape[0]
    fold_ref[pl.ds((c // 8) * rows * 8 + c % 8, rows, stride=8), :] = values


def get_tail(fold_ref, c, rows):
    return fold_ref[pl.ds((c // 8) * rows * 8 + c % 8, rows, stride=8), :].astype(BF16)


def store_tail(out_ref, fold_ref, blocks, tail):
    experts = out_ref.shape[0]
    span = experts * tail * 8
    for group in range(blocks // 8):
        first = blocks + group * tail
        out_ref[:, first : first + tail, :, :] = (
            fold_ref[group * span : (group + 1) * span, :].reshape(experts, tail, 8, LANES).astype(BF16)
        )


def load_tail(in_ref, fold_ref, blocks, tail):
    experts = in_ref.shape[0]
    span = experts * tail * 8
    for group in range(blocks // 8):
        first = blocks + group * tail
        fold_ref[group * span : (group + 1) * span, :] = (
            in_ref[:, first : first + tail, :, :].astype(F32).reshape(span, LANES)
        )


def pack_kernel(tail, routes_ref, x_ref, out_ref, fold_ref):
    experts = out_ref.shape[0]
    tokens, width = x_ref.shape
    blocks = width // LANES
    routes = routes_ref[...]
    expert_id = lax.broadcasted_iota(jnp.int32, (experts, tokens), 0)
    earlier = lax.broadcasted_iota(jnp.int32, (tokens, tokens), 0) < lax.broadcasted_iota(
        jnp.int32, (tokens, tokens), 1
    )
    earlier = earlier.astype(F32).astype(BF16)
    seen = jnp.zeros((experts, 1), F32)
    picks = []
    for k in range(routes.shape[0]):
        route = routes[k : k + 1, :]
        hit = (expert_id == route).astype(F32)
        ahead = jnp.dot(hit.astype(BF16), earlier, preferred_element_type=F32) + seen
        rank = jnp.sum(hit * ahead, axis=0, keepdims=True).astype(jnp.int32)
        seen = seen + jnp.sum(hit, axis=1, keepdims=True)
        picks.append((route, rank))
    head_row = lax.broadcasted_iota(jnp.int32, (experts * HEAD, tokens), 0)
    tail_row = lax.broadcasted_iota(jnp.int32, (experts * tail, tokens), 0)
    head_pick = jnp.zeros(head_row.shape, F32)
    tail_pick = jnp.zeros(tail_row.shape, F32)
    for route, rank in picks:
        head_place = jnp.where(rank < HEAD, route * HEAD + rank, -1)
        tail_place = jnp.where(rank >= HEAD, route * tail + rank - HEAD, -1)
        head_pick = head_pick + (head_row == head_place).astype(F32)
        tail_pick = tail_pick + (tail_row == tail_place).astype(F32)
    head_pick = head_pick.astype(BF16)
    tail_pick = tail_pick.astype(BF16)
    for c in range(0, blocks, 2):
        columns = x_ref[:, c * LANES : (c + 2) * LANES]
        rows = jnp.dot(head_pick, columns, preferred_element_type=F32)
        put_head(out_ref, c, rows[:, :LANES])
        put_head(out_ref, c + 1, rows[:, LANES:])
        rows = jnp.dot(tail_pick, columns, preferred_element_type=F32)
        put_tail(fold_ref, c, rows[:, :LANES])
        put_tail(fold_ref, c + 1, rows[:, LANES:])
    store_tail(out_ref, fold_ref, blocks, tail)


def pack(routes_t, x, experts, tail):
    blocks = x.shape[1] // LANES
    tiles = blocks + blocks // 8 * tail
    (out,) = kernel_call(
        lambda *refs: pack_kernel(tail, *refs),
        [((experts, tiles, 8, LANES), BF16)],
        [VMEM, VMEM],
        (routes_t, x),
        [pltpu.VMEM((blocks * experts * tail, LANES), F32)],
    )
    return out


def down_half(tail, hidden, wd_ref, downs, out_ref, fold_ref):
    experts = out_ref.shape[0]
    pairs = wd_ref.shape[0] // 2
    for p in range(pairs):
        for copy in downs[2 * p : 2 * p + 2]:
            copy.wait()
        pair = (wd_ref[2 * p], wd_ref[2 * p + 1])
        weight = jnp.concatenate(
            [jnp.concatenate([w[:, lane_block(h)] for w in pair], axis=1) for h in range(2)], axis=0
        )
        rows = jnp.dot(hidden, weight, preferred_element_type=F32)
        for j in range(2):
            put_head(out_ref, 2 * p + j, rows[: experts * HEAD, lane_block(j)])
            put_tail(fold_ref, 2 * p + j, rows[experts * HEAD :, lane_block(j)])
    store_tail(out_ref, fold_ref, 2 * pairs, tail)


def down_copies(w_ref, base, wd_ref, sems):
    reps, half, _ = wd_ref.shape
    return [
        pltpu.make_async_copy(w_ref.at[r, pl.ds(base, half)], wd_ref.at[r], sems.at[r]) for r in range(reps)
    ]


def unfold_kernel(tail, in_ref, rows_ref, fold_ref):
    reps, count, depth = rows_ref.shape
    first = in_ref.shape[0] * HEAD
    load_tail(in_ref, fold_ref, reps * depth // LANES, tail)
    for c in range(reps * depth // LANES):
        r, lanes = c * LANES // depth, lane_block(c % (depth // LANES))
        rows_ref[r, :first, lanes] = get_head(in_ref, c)
        rows_ref[r, first:, lanes] = get_tail(fold_ref, c, count - first)


def expert_kernel(
    tail, in_ref, w_ref, hid_ref, out_ref, rows_ref, wv_ref, wd_ref, fold_ref, row_sems, sems, down_sems
):
    reps, wide, depth = wv_ref.shape
    ff = wide // 2
    count = rows_ref.shape[1]
    copies = []
    for r in range(reps):
        copies.append(
            (
                pltpu.make_async_copy(in_ref.at[r], rows_ref.at[r], row_sems.at[r]),
                pltpu.make_async_copy(w_ref.at[r, pl.ds(0, wide)], wv_ref.at[r], sems.at[r]),
            )
        )
    downs = down_copies(w_ref, wide, wd_ref, down_sems)
    for pair in copies:
        for copy in pair:
            copy.start()
    for copy in downs:
        copy.start()
    step = count // 2
    sums = [None] * 4
    for r in range(reps):
        for copy in copies[r]:
            copy.wait()
        for i in range(4):
            rows = rows_ref[r, (i // 2) * step : (i // 2 + 1) * step, :]
            weight = wv_ref[r, (i % 2) * ff : (i % 2 + 1) * ff, :]
            part = lax.dot_general(rows, weight, NT, preferred_element_type=F32)
            sums[i] = part if r == 0 else sums[i] + part
    for i in range(2):
        gate, up = sums[2 * i], sums[2 * i + 1]
        hid_ref[i * step : (i + 1) * step, :] = (gate / (1.0 + jnp.exp(-gate)) * up).astype(BF16)
    down_half(tail, hid_ref[...], wd_ref, downs, out_ref, fold_ref)


def second_kernel(tail, hid_ref, w_ref, out_ref, wd_ref, fold_ref, down_sems):
    downs = down_copies(w_ref, 0, wd_ref, down_sems)
    for copy in downs:
        copy.start()
    down_half(tail, hid_ref[...], wd_ref, downs, out_ref, fold_ref)


def mix_half(half, back_ref, mix_ref, base_ref, fold_ref, tail, store):
    experts = back_ref.shape[0]
    blocks = base_ref.shape[1] // (2 * LANES)
    first = experts * HEAD
    load_tail(back_ref, fold_ref, blocks, tail)
    for p in range(blocks // 2):
        cs = (2 * p, 2 * p + 1)
        head = jnp.concatenate([get_head(back_ref, c) for c in cs], axis=1)
        rest = jnp.concatenate([get_tail(fold_ref, c, experts * tail) for c in cs], axis=1)
        added = sum(
            jnp.dot(mix_ref[i, :, :first], head, preferred_element_type=F32)
            + jnp.dot(mix_ref[i, :, first:], rest, preferred_element_type=F32)
            for i in range(2)
        )
        for j, c in enumerate(cs):
            columns = lane_block(2 * c + half)
            store(columns, (base_ref[:, columns].astype(F32) + added[:, lane_block(j)]).astype(BF16))


def mix_kernel(tail, back_ref, mix_ref, x_ref, out_ref, fold_ref):
    def store(columns, value):
        out_ref[:, columns] = value

    for c in range(1, x_ref.shape[1] // LANES, 2):
        out_ref[:, lane_block(c)] = x_ref[:, lane_block(c)]
    mix_half(0, back_ref, mix_ref, x_ref, fold_ref, tail, store)


def score_kernel(tail, gain, hit_ref, back_ref, mix_ref, base_ref, proj_ref, query_ref, *refs):
    states_out_ref, states_ref, weights_ref, unit_ref, radius_ref, totals_ref, logits_ref, shares_ref = refs[:8]
    fold_ref, out_sem = refs[8:]

    def store(columns, value):
        states_ref[:, columns] = value

    for c in range(0, base_ref.shape[1] // LANES, 2):
        states_ref[:, lane_block(c)] = base_ref[:, lane_block(c)]
    mix_half(1, back_ref, mix_ref, base_ref, fold_ref, tail, store)
    copy_out = pltpu.make_async_copy(states_ref, states_out_ref, out_sem)
    copy_out.start()
    projected = jnp.dot(states_ref[...], proj_ref[...], preferred_element_type=F32)
    radius = jnp.sqrt(jnp.sum(projected * projected, axis=1, keepdims=True) + norm_eps)
    unit = projected / radius
    unit_ref[...] = unit
    radius_ref[...] = jnp.broadcast_to(radius, radius_ref.shape)
    unit_vec = unit.astype(BF16)
    step = 4 * LANES
    logits = jnp.zeros((1, LANES), F32)
    for n in range(0, query_ref.shape[0], step):
        scores = lax.dot_general(unit_vec, query_ref[n : n + step, :], NT, preferred_element_type=F32)
        weights = jnp.exp(scores * (1.0 / soft_temp))
        weights_ref[:, n : n + step] = weights
        totals = jnp.sum(weights, axis=0, keepdims=True)
        totals_ref[:, n : n + step] = totals
        logs = soft_temp * jnp.log(totals)
        for j in range(step // LANES):
            logits = logits + logs[:, lane_block(j)]
    logits = gain * logits
    logits_ref[...] = logits
    held = jnp.where(lax.broadcasted_iota(jnp.int32, logits.shape, 1) == hit_ref[0, 0], logits, 0.0)
    odd = lax.broadcasted_iota(jnp.int32, shares_ref.shape, 0) % 2
    shares_ref[...] = jnp.where(odd == 0, jnp.exp(logits), held)
    copy_out.wait()


def grad_kernel(
    gain, hit_ref, sums_ref, logits_ref, weights_ref, totals_ref, query_ref, unit_ref, radius_ref,
    states_ref, share_ref, loss_ref,
):
    step = 4 * LANES
    senders = sums_ref.shape[0] // 2
    partition = jnp.sum(sums_ref[pl.ds(0, senders, stride=2), :], axis=0, keepdims=True)
    held = jnp.sum(sums_ref[pl.ds(1, senders, stride=2), :], axis=0, keepdims=True)
    loss = jnp.sum(jnp.log(partition) - held, axis=1, keepdims=True) / partition.shape[1]
    loss_ref[...] = jnp.broadcast_to(loss, loss_ref.shape)
    positive = (lax.broadcasted_iota(jnp.int32, partition.shape, 1) == hit_ref[0, 0]).astype(F32)
    factor = gain * (jnp.exp(logits_ref[...]) / partition - positive)
    grad = None
    for n in range(0, query_ref.shape[0], step):
        scale = jnp.concatenate([factor] * (step // LANES), axis=1) / totals_ref[:, n : n + step]
        coeffs = (weights_ref[:, n : n + step] * scale).astype(BF16)
        part = jnp.dot(coeffs, query_ref[n : n + step, :], preferred_element_type=F32)
        grad = part if grad is None else grad + part
    unit = unit_ref[...]
    along = jnp.sum(unit * grad, axis=1, keepdims=True)
    grad_vec = ((grad - unit * along) / radius_ref[...]).astype(BF16)
    share_ref[...] = lax.dot_general(
        states_ref[...], grad_vec, (((0,), (0,)), ((), ())), preferred_element_type=F32
    ).astype(BF16)


def join_kernel(gate_ref, up_ref, down_ref, out_ref):
    ff = gate_ref.shape[0]
    half = ff // 2
    out_ref[:ff, :] = gate_ref[...]
    out_ref[ff : 2 * ff, :] = up_ref[...]
    out_ref[2 * ff :, :LANES] = down_ref[:half, :LANES]
    out_ref[2 * ff :, LANES:] = down_ref[half:, :LANES]


def fan_kernel(copies, in_ref, out_ref):
    rows = in_ref.shape[0] // 2
    even = jnp.sum(in_ref[pl.ds(0, rows, stride=2), :], axis=0, keepdims=True)
    odd = jnp.sum(in_ref[pl.ds(1, rows, stride=2), :], axis=0, keepdims=True)
    parity = lax.broadcasted_iota(jnp.int32, out_ref.shape, 0) % 2
    out_ref[...] = jnp.where(parity == 0, even, odd)


def body(
    passages_in,
    routes,
    route_weights,
    gate_weight,
    up_weight,
    down_weight,
    projection,
    queries,
    positives,
):
    tok_count, model_width = passages_in.shape
    top_count = routes.shape[1]
    experts = lax.axis_size("exp")
    rep_count = lax.axis_size("rep")
    ff = gate_weight.shape[2]
    capacity = max(2, 2 * tok_count * top_count // experts)
    tail = capacity - HEAD
    slots = experts * capacity
    blocks = model_width // LANES
    fold = experts * tail * 8

    down = down_weight[0]
    (first_part,) = kernel_call(
        join_kernel,
        [((5 * ff // 2, 2 * LANES), BF16)],
        [VMEM] * 3,
        (gate_weight[0].T, up_weight[0].T, down),
        room=56,
    )
    first_all = lax.all_gather(first_part, "rep", axis=0, tiled=False)
    wide_queries = queries.astype(F32)
    query_radius = jnp.sqrt(jnp.sum(wide_queries * wide_queries, axis=-1, keepdims=True) + norm_eps)
    query_unit = (wide_queries / query_radius).astype(BF16)
    query_block, query_len, unit_width = queries.shape
    total_queries = query_block * rep_count
    own_rows = query_unit.transpose(1, 0, 2).reshape(query_len * query_block, unit_width)
    own_half = own_rows.shape[0] // 2
    second_part = jnp.concatenate(
        [
            jnp.concatenate([down[: ff // 2, LANES:], own_rows[:own_half]], axis=0),
            jnp.concatenate([down[ff // 2 :, LANES:], own_rows[own_half:]], axis=0),
        ],
        axis=1,
    )
    second_all = lax.all_gather(second_part, "rep", axis=0, tiled=False)
    query_rows = (
        jnp.concatenate([second_all[:, ff // 2 :, lane_block(h)] for h in range(2)], axis=1)
        .reshape(rep_count, query_len, query_block, unit_width)
        .transpose(1, 0, 2, 3)
        .reshape(query_len * total_queries, unit_width)
    )

    def exchange(tiles):
        return lax.all_to_all(tiles, "exp", split_axis=0, concat_axis=0, tiled=True)

    packed = pack(routes.T, passages_in, experts, tail)
    arrived = exchange(packed)

    (rows_in,) = kernel_call(
        lambda *refs: unfold_kernel(tail, *refs),
        [((rep_count, slots, model_width // rep_count), BF16)],
        [VMEM],
        (arrived,),
        [pltpu.VMEM((2 * fold, LANES), F32)],
        room=56,
    )
    half_tiles = ((experts, blocks // 2 + blocks // 16 * tail, 8, LANES), BF16)
    depth = model_width // rep_count
    down_room = pltpu.VMEM((rep_count, ff // 2, 2 * LANES), BF16)
    fold_room = pltpu.VMEM((fold, LANES), F32)
    copy_sems = pltpu.SemaphoreType.DMA
    hidden, send_a = kernel_call(
        lambda *refs: expert_kernel(tail, *refs),
        [((slots, ff), BF16), half_tiles],
        [HBM, HBM],
        (rows_in, first_all),
        [pltpu.VMEM((rep_count, slots, depth), BF16), pltpu.VMEM((rep_count, 2 * ff, depth), BF16)]
        + [down_room, fold_room]
        + [copy_sems((rep_count,))] * 3,
        room=56,
    )
    back_a = exchange(send_a)
    (send_b,) = kernel_call(
        lambda *refs: second_kernel(tail, *refs),
        [half_tiles],
        [VMEM, HBM],
        (hidden, second_all),
        [down_room, fold_room, copy_sems((rep_count,))],
        room=56,
    )
    back_b = exchange(send_b)

    later_routes, _ = lax.optimization_barrier((routes, packed))
    flat = later_routes.T.reshape(-1)
    count = flat.shape[0]
    onehot = flat[:, None] == jnp.arange(experts, dtype=jnp.int32)[None, :]
    before = jnp.arange(count)[:, None] > jnp.arange(count)[None, :]
    earlier = jnp.dot(before.astype(BF16), onehot.astype(BF16), preferred_element_type=F32)
    rank = jnp.sum(jnp.where(onehot, earlier, 0.0), axis=1).astype(jnp.int32)
    place = jnp.where(rank < HEAD, flat * HEAD + rank, experts * HEAD + flat * tail + rank - HEAD)
    place = place.reshape(top_count, tok_count)
    hit = place[:, :, None] == jnp.arange(slots, dtype=jnp.int32)[None, None, :]
    mix = jnp.sum(jnp.where(hit, route_weights.T[:, :, None], 0.0), axis=0)
    high = mix.astype(BF16)
    low = (mix - high.astype(F32)).astype(BF16)
    mix_parts = jnp.stack([high, low])

    owner = lax.axis_index(("exp", "rep")).astype(jnp.int32)
    hit_query = jnp.max(jnp.where(positives == owner, jnp.arange(total_queries, dtype=jnp.int32), -1)).reshape(1, 1)

    (base,) = kernel_call(
        lambda *refs: mix_kernel(tail, *refs),
        [((tok_count, model_width), BF16)],
        [VMEM] * 3,
        (back_a, mix_parts, passages_in),
        [fold_room],
        room=56,
    )
    columns = query_len * total_queries
    states, states_near, weights, unit, radius, totals, logits, shares = kernel_call(
        lambda *refs: score_kernel(tail, logit_gain, *refs),
        [
            ((tok_count, model_width), BF16),
            ((tok_count, model_width), BF16),
            ((tok_count, columns), F32),
            ((tok_count, unit_width), F32),
            ((tok_count, unit_width), F32),
            ((1, columns), F32),
            ((1, total_queries), F32),
            ((2 * experts, total_queries), F32),
        ],
        [SMEM] + [VMEM] * 5,
        (hit_query, back_b, mix_parts, base, projection, query_rows),
        [fold_room, copy_sems],
        room=24,
        out_specs=[HBM] + [VMEM] * 7,
    )

    def share_out(rows, axis):
        pairs = rows.reshape(-1, 2, total_queries)
        return lax.all_to_all(pairs, axis, split_axis=0, concat_axis=0, tiled=True).reshape(rows.shape)

    (fanned,) = kernel_call(
        lambda *refs: fan_kernel(rep_count, *refs),
        [((2 * rep_count, total_queries), F32)],
        [VMEM],
        (share_out(shares, "exp"),),
    )
    sums = share_out(fanned, "rep")
    share, loss = kernel_call(
        lambda *refs: grad_kernel(logit_gain, *refs),
        [((model_width, unit_width), BF16), ((1, LANES), F32)],
        [SMEM] + [VMEM] * 8,
        (hit_query, sums, logits, weights, totals, query_rows, unit, radius, states_near),
        room=24,
    )
    rows_out = model_width // experts
    parts = exchange(share.reshape(experts, rows_out, unit_width))
    part_sum = jnp.sum(parts.astype(F32), axis=0)
    sent = jnp.broadcast_to(part_sum[None], (rep_count,) + part_sum.shape)
    grad_projection = jnp.sum(lax.all_to_all(sent, "rep", split_axis=0, concat_axis=0, tiled=True), axis=0)
    return (states, grad_projection, loss[0, 0])


def solution(mesh):
    in_specs = (
        P(("exp", "rep"), None),
        P(("exp", "rep"), None),
        P(("exp", "rep"), None),
        P("exp", "rep", None),
        P("exp", "rep", None),
        P("exp", None, "rep"),
        P(),
        P("rep", None, None),
        P(),
    )
    out_specs = (P(("exp", "rep"), None), P("exp", None), P())
    return jax.shard_map(body, mesh=mesh, in_specs=in_specs, out_specs=out_specs, check_vma=False)
```

```python
import jax
import jax.numpy as jnp
from jax import lax
from jax.experimental import pallas as pl
from jax.experimental.pallas import tpu as pltpu
from jax.sharding import PartitionSpec as P

HEAD = 8
LANES = 128

soft_temp = 0.05
logit_gain = 1.5
norm_eps = 1e-06
F32 = jnp.float32
BF16 = jnp.bfloat16
NT = (((1,), (1,)), ((), ()))
VMEM = pl.BlockSpec(memory_space=pltpu.VMEM)
HBM = pl.BlockSpec(memory_space=pl.ANY)
SMEM = pl.BlockSpec(memory_space=pltpu.SMEM)


def kernel_call(kernel, outs, ins, args, scratch=(), room=24, out_specs=None):
    return pl.pallas_call(
        kernel,
        in_specs=ins,
        out_specs=out_specs or [VMEM] * len(outs),
        out_shape=[jax.ShapeDtypeStruct(*o) for o in outs],
        scratch_shapes=scratch,
        compiler_params=pltpu.CompilerParams(vmem_limit_bytes=room * 2**20),
    )(*args)


def lane_block(c):
    return slice(c * LANES, (c + 1) * LANES)


def put_head(out_ref, c, values):
    out_ref[:, c, :, :] = values.reshape(-1, HEAD, LANES).astype(BF16)


def get_head(in_ref, c):
    return in_ref[:, c, :, :].astype(F32).reshape(-1, LANES).astype(BF16)


def put_tail(fold_ref, c, values):
    rows = values.shape[0]
    fold_ref[pl.ds((c // 8) * rows * 8 + c % 8, rows, stride=8), :] = values


def get_tail(fold_ref, c, rows):
    return fold_ref[pl.ds((c // 8) * rows * 8 + c % 8, rows, stride=8), :].astype(BF16)


def store_tail(out_ref, fold_ref, blocks, tail):
    experts = out_ref.shape[0]
    span = experts * tail * 8
    for group in range(blocks // 8):
        first = blocks + group * tail
        out_ref[:, first : first + tail, :, :] = (
            fold_ref[group * span : (group + 1) * span, :].reshape(experts, tail, 8, LANES).astype(BF16)
        )


def load_tail(in_ref, fold_ref, blocks, tail):
    experts = in_ref.shape[0]
    span = experts * tail * 8
    for group in range(blocks // 8):
        first = blocks + group * tail
        fold_ref[group * span : (group + 1) * span, :] = (
            in_ref[:, first : first + tail, :, :].astype(F32).reshape(span, LANES)
        )


def pack_kernel(tail, routes_ref, x_ref, out_ref, fold_ref):
    experts = out_ref.shape[0]
    tokens, width = x_ref.shape
    blocks = width // LANES
    routes = routes_ref[...]
    expert_id = lax.broadcasted_iota(jnp.int32, (experts, tokens), 0)
    earlier = lax.broadcasted_iota(jnp.int32, (tokens, tokens), 0) < lax.broadcasted_iota(
        jnp.int32, (tokens, tokens), 1
    )
    earlier = earlier.astype(F32).astype(BF16)
    seen = jnp.zeros((experts, 1), F32)
    picks = []
    for k in range(routes.shape[0]):
        route = routes[k : k + 1, :]
        hit = (expert_id == route).astype(F32)
        ahead = jnp.dot(hit.astype(BF16), earlier, preferred_element_type=F32) + seen
        rank = jnp.sum(hit * ahead, axis=0, keepdims=True).astype(jnp.int32)
        seen = seen + jnp.sum(hit, axis=1, keepdims=True)
        picks.append((route, rank))
    head_row = lax.broadcasted_iota(jnp.int32, (experts * HEAD, tokens), 0)
    tail_row = lax.broadcasted_iota(jnp.int32, (experts * tail, tokens), 0)
    head_pick = jnp.zeros(head_row.shape, F32)
    tail_pick = jnp.zeros(tail_row.shape, F32)
    for route, rank in picks:
        head_place = jnp.where(rank < HEAD, route * HEAD + rank, -1)
        tail_place = jnp.where(rank >= HEAD, route * tail + rank - HEAD, -1)
        head_pick = head_pick + (head_row == head_place).astype(F32)
        tail_pick = tail_pick + (tail_row == tail_place).astype(F32)
    head_pick = head_pick.astype(BF16)
    tail_pick = tail_pick.astype(BF16)
    for c in range(0, blocks, 2):
        columns = x_ref[:, c * LANES : (c + 2) * LANES]
        rows = jnp.dot(head_pick, columns, preferred_element_type=F32)
        put_head(out_ref, c, rows[:, :LANES])
        put_head(out_ref, c + 1, rows[:, LANES:])
        rows = jnp.dot(tail_pick, columns, preferred_element_type=F32)
        put_tail(fold_ref, c, rows[:, :LANES])
        put_tail(fold_ref, c + 1, rows[:, LANES:])
    store_tail(out_ref, fold_ref, blocks, tail)


def pack(routes_t, x, experts, tail):
    blocks = x.shape[1] // LANES
    tiles = blocks + blocks // 8 * tail
    (out,) = kernel_call(
        lambda *refs: pack_kernel(tail, *refs),
        [((experts, tiles, 8, LANES), BF16)],
        [VMEM, VMEM],
        (routes_t, x),
        [pltpu.VMEM((blocks * experts * tail, LANES), F32)],
    )
    return out


def down_half(tail, hidden, wd_ref, downs, out_ref, fold_ref):
    experts = out_ref.shape[0]
    pairs = wd_ref.shape[0] // 2
    for copy in downs:
        copy.wait()
    for p in range(pairs):
        pair = (wd_ref[2 * p], wd_ref[2 * p + 1])
        weight = jnp.concatenate(
            [jnp.concatenate([w[:, lane_block(h)] for w in pair], axis=1) for h in range(2)], axis=0
        )
        rows = jnp.dot(hidden, weight, preferred_element_type=F32)
        for j in range(2):
            put_head(out_ref, 2 * p + j, rows[: experts * HEAD, lane_block(j)])
            put_tail(fold_ref, 2 * p + j, rows[experts * HEAD :, lane_block(j)])
    store_tail(out_ref, fold_ref, 2 * pairs, tail)


def down_copies(w_ref, base, wd_ref, sems):
    reps, half, _ = wd_ref.shape
    return [
        pltpu.make_async_copy(w_ref.at[r, pl.ds(base, half)], wd_ref.at[r], sems.at[r]) for r in range(reps)
    ]


def unfold_kernel(tail, in_ref, rows_ref, fold_ref):
    reps, count, depth = rows_ref.shape
    first = in_ref.shape[0] * HEAD
    load_tail(in_ref, fold_ref, reps * depth // LANES, tail)
    for c in range(reps * depth // LANES):
        r, lanes = c * LANES // depth, lane_block(c % (depth // LANES))
        rows_ref[r, :first, lanes] = get_head(in_ref, c)
        rows_ref[r, first:, lanes] = get_tail(fold_ref, c, count - first)


def expert_kernel(
    tail, in_ref, w_ref, far_ref, out_ref, rows_ref, hid_ref, wv_ref, wd_ref, fold_ref, row_sems, sems, down_sems, hid_sem
):
    reps, wide, depth = wv_ref.shape
    ff = wide // 2
    count = rows_ref.shape[1]
    copies = []
    for r in range(reps):
        copies.append(
            (
                pltpu.make_async_copy(in_ref.at[r], rows_ref.at[r], row_sems.at[r]),
                pltpu.make_async_copy(w_ref.at[r, pl.ds(0, wide)], wv_ref.at[r], sems.at[r]),
            )
        )
    downs = down_copies(w_ref, wide, wd_ref, down_sems)
    sizes = (2, 3, 3)
    firsts = [sum(sizes[:i]) for i in range(len(sizes))]
    queue = [sum(copies[r : r + n], ()) for r, n in zip(firsts, sizes)] + [downs]
    ahead = 2
    for group in queue[:ahead]:
        for copy in group:
            copy.start()
    step = count // 2
    sums = [None] * 4
    for r in range(reps):
        if r in firsts:
            for copy in queue[firsts.index(r)]:
                copy.wait()
            for group in queue[firsts.index(r) + ahead :][:1]:
                for copy in group:
                    copy.start()
        for i in range(4):
            rows = rows_ref[r, (i // 2) * step : (i // 2 + 1) * step, :]
            weight = wv_ref[r, (i % 2) * ff : (i % 2 + 1) * ff, :]
            part = lax.dot_general(rows, weight, NT, preferred_element_type=F32)
            sums[i] = part if r == 0 else sums[i] + part
    for i in range(2):
        gate, up = sums[2 * i], sums[2 * i + 1]
        hid_ref[i * step : (i + 1) * step, :] = (gate / (1.0 + jnp.exp(-gate)) * up).astype(BF16)
    kept = pltpu.make_async_copy(hid_ref, far_ref, hid_sem)
    kept.start()
    down_half(tail, hid_ref[...], wd_ref, downs, out_ref, fold_ref)
    kept.wait()


def second_kernel(tail, hid_ref, w_ref, out_ref, wd_ref, fold_ref, down_sems):
    downs = down_copies(w_ref, 0, wd_ref, down_sems)
    for copy in downs:
        copy.start()
    down_half(tail, hid_ref[...], wd_ref, downs, out_ref, fold_ref)


def part_rows(rows):
    return (rows + 63) // 64 * 64


def mix_half(half, back_ref, mix_ref, base_ref, fold_ref, tail, store):
    tokens = base_ref.shape[0]
    spread = part_rows(tokens)
    experts = back_ref.shape[0]
    blocks = base_ref.shape[1] // (2 * LANES)
    first = experts * HEAD
    load_tail(back_ref, fold_ref, blocks, tail)
    for p in range(blocks // 2):
        cs = (2 * p, 2 * p + 1)
        head = jnp.concatenate([get_head(back_ref, c) for c in cs], axis=1)
        rest = jnp.concatenate([get_tail(fold_ref, c, experts * tail) for c in cs], axis=1)
        added = sum(
            jnp.dot(mix_ref[i * spread : i * spread + tokens, :first], head, preferred_element_type=F32)
            + jnp.dot(mix_ref[i * spread : i * spread + tokens, first:], rest, preferred_element_type=F32)
            for i in range(2)
        )
        for j, c in enumerate(cs):
            columns = lane_block(2 * c + half)
            store(columns, (base_ref[:, columns].astype(F32) + added[:, lane_block(j)]).astype(BF16))


def mix_kernel(tail, back_ref, mix_ref, x_ref, out_ref, fold_ref):
    def store(columns, value):
        out_ref[:, columns] = value

    for c in range(1, x_ref.shape[1] // LANES, 2):
        out_ref[:, lane_block(c)] = x_ref[:, lane_block(c)]
    mix_half(0, back_ref, mix_ref, x_ref, fold_ref, tail, store)


def score_kernel(tail, gain, hit_ref, back_ref, mix_ref, base_ref, query_ref, *refs):
    states_out_ref, states_ref, weights_ref, unit_ref, radius_ref, totals_ref, logits_ref, shares_ref = refs[:8]
    fold_ref, out_sem = refs[8:]

    def store(columns, value):
        states_ref[:, columns] = value

    for c in range(0, base_ref.shape[1] // LANES, 2):
        states_ref[:, lane_block(c)] = base_ref[:, lane_block(c)]
    mix_half(1, back_ref, mix_ref, base_ref, fold_ref, tail, store)
    copy_out = pltpu.make_async_copy(states_ref, states_out_ref, out_sem)
    copy_out.start()
    first = 2 * part_rows(states_ref.shape[0])
    depth = mix_ref.shape[0] - first
    projected = sum(
        jnp.dot(
            states_ref[:, b * depth : (b + 1) * depth], mix_ref[first:, lane_block(b)], preferred_element_type=F32
        )
        for b in range(states_ref.shape[1] // depth)
    )
    radius = jnp.sqrt(jnp.sum(projected * projected, axis=1, keepdims=True) + norm_eps)
    unit = projected / radius
    unit_ref[...] = unit
    radius_ref[...] = jnp.broadcast_to(radius, radius_ref.shape)
    unit_vec = unit.astype(BF16)
    step = 4 * LANES
    logits = jnp.zeros((1, LANES), F32)
    for n in range(0, query_ref.shape[0], step):
        scores = lax.dot_general(unit_vec, query_ref[n : n + step, :], NT, preferred_element_type=F32)
        weights = jnp.exp(scores * (1.0 / soft_temp))
        weights_ref[:, n : n + step] = weights
        totals = jnp.sum(weights, axis=0, keepdims=True)
        totals_ref[:, n : n + step] = totals
        logs = soft_temp * jnp.log(totals)
        for j in range(step // LANES):
            logits = logits + logs[:, lane_block(j)]
    logits = gain * logits
    logits_ref[...] = logits
    held = jnp.where(lax.broadcasted_iota(jnp.int32, logits.shape, 1) == hit_ref[0, 0], logits, 0.0)
    odd = lax.broadcasted_iota(jnp.int32, shares_ref.shape, 0) % 2
    shares_ref[...] = jnp.where(odd == 0, jnp.exp(logits), held)
    copy_out.wait()


def grad_kernel(
    gain, hit_ref, sums_ref, logits_ref, weights_ref, totals_ref, query_ref, unit_ref, radius_ref,
    states_ref, share_ref, loss_ref,
):
    step = 4 * LANES
    senders = sums_ref.shape[0] // 2
    partition = jnp.sum(sums_ref[pl.ds(0, senders, stride=2), :], axis=0, keepdims=True)
    held = jnp.sum(sums_ref[pl.ds(1, senders, stride=2), :], axis=0, keepdims=True)
    loss = jnp.sum(jnp.log(partition) - held, axis=1, keepdims=True) / partition.shape[1]
    loss_ref[...] = jnp.broadcast_to(loss, loss_ref.shape)
    positive = (lax.broadcasted_iota(jnp.int32, partition.shape, 1) == hit_ref[0, 0]).astype(F32)
    factor = gain * (jnp.exp(logits_ref[...]) / partition - positive)
    grad = None
    for n in range(0, query_ref.shape[0], step):
        scale = jnp.concatenate([factor] * (step // LANES), axis=1) / totals_ref[:, n : n + step]
        coeffs = (weights_ref[:, n : n + step] * scale).astype(BF16)
        part = jnp.dot(coeffs, query_ref[n : n + step, :], preferred_element_type=F32)
        grad = part if grad is None else grad + part
    unit = unit_ref[...]
    along = jnp.sum(unit * grad, axis=1, keepdims=True)
    grad_vec = ((grad - unit * along) / radius_ref[...]).astype(BF16)
    share_ref[...] = lax.dot_general(
        states_ref[...], grad_vec, (((0,), (0,)), ((), ())), preferred_element_type=F32
    ).astype(BF16)


def join_kernel(gate_ref, up_ref, down_ref, out_ref):
    ff = gate_ref.shape[0]
    half = ff // 2
    out_ref[:ff, :] = gate_ref[...]
    out_ref[ff : 2 * ff, :] = up_ref[...]
    out_ref[2 * ff :, :LANES] = down_ref[:half, :LANES]
    out_ref[2 * ff :, LANES:] = down_ref[half:, :LANES]


def fan_kernel(copies, in_ref, out_ref):
    rows = in_ref.shape[0] // 2
    even = jnp.sum(in_ref[pl.ds(0, rows, stride=2), :], axis=0, keepdims=True)
    odd = jnp.sum(in_ref[pl.ds(1, rows, stride=2), :], axis=0, keepdims=True)
    parity = lax.broadcasted_iota(jnp.int32, out_ref.shape, 0) % 2
    out_ref[...] = jnp.where(parity == 0, even, odd)


def body(
    passages_in,
    routes,
    route_weights,
    gate_weight,
    up_weight,
    down_weight,
    projection,
    queries,
    positives,
):
    tok_count, model_width = passages_in.shape
    top_count = routes.shape[1]
    experts = lax.axis_size("exp")
    rep_count = lax.axis_size("rep")
    ff = gate_weight.shape[2]
    capacity = max(2, 2 * tok_count * top_count // experts)
    tail = capacity - HEAD
    slots = experts * capacity
    blocks = model_width // LANES
    fold = experts * tail * 8

    down = down_weight[0]
    (first_part,) = kernel_call(
        join_kernel,
        [((5 * ff // 2, 2 * LANES), BF16)],
        [VMEM] * 3,
        (gate_weight[0].T, up_weight[0].T, down),
        room=56,
    )
    first_all = lax.all_gather(first_part, "rep", axis=0, tiled=False)
    wide_queries = queries.astype(F32)
    query_radius = jnp.sqrt(jnp.sum(wide_queries * wide_queries, axis=-1, keepdims=True) + norm_eps)
    query_unit = (wide_queries / query_radius).astype(BF16)
    query_block, query_len, unit_width = queries.shape
    total_queries = query_block * rep_count
    own_rows = query_unit.transpose(1, 0, 2).reshape(query_len * query_block, unit_width)
    own_half = own_rows.shape[0] // 2
    second_part = jnp.concatenate(
        [
            jnp.concatenate([down[: ff // 2, LANES:], own_rows[:own_half]], axis=0),
            jnp.concatenate([down[ff // 2 :, LANES:], own_rows[own_half:]], axis=0),
        ],
        axis=1,
    )
    second_all = lax.all_gather(second_part, "rep", axis=0, tiled=False)
    query_rows = (
        jnp.concatenate([second_all[:, ff // 2 :, lane_block(h)] for h in range(2)], axis=1)
        .reshape(rep_count, query_len, query_block, unit_width)
        .transpose(1, 0, 2, 3)
        .reshape(query_len * total_queries, unit_width)
    )

    def exchange(tiles):
        return lax.all_to_all(tiles, "exp", split_axis=0, concat_axis=0, tiled=True)

    packed = pack(routes.T, passages_in, experts, tail)
    arrived = exchange(packed)

    (rows_in,) = kernel_call(
        lambda *refs: unfold_kernel(tail, *refs),
        [((rep_count, slots, model_width // rep_count), BF16)],
        [VMEM],
        (arrived,),
        [pltpu.VMEM((2 * fold, LANES), F32)],
        room=56,
    )
    half_tiles = ((experts, blocks // 2 + blocks // 16 * tail, 8, LANES), BF16)
    depth = model_width // rep_count
    down_room = pltpu.VMEM((rep_count, ff // 2, 2 * LANES), BF16)
    fold_room = pltpu.VMEM((fold, LANES), F32)
    copy_sems = pltpu.SemaphoreType.DMA
    hidden, send_a = kernel_call(
        lambda *refs: expert_kernel(tail, *refs),
        [((slots, ff), BF16), half_tiles],
        [HBM, HBM],
        (rows_in, first_all),
        [pltpu.VMEM((rep_count, slots, depth), BF16), pltpu.VMEM((slots, ff), BF16)]
        + [pltpu.VMEM((rep_count, 2 * ff, depth), BF16), down_room, fold_room]
        + [copy_sems((rep_count,))] * 3
        + [copy_sems],
        room=56,
        out_specs=[HBM, VMEM],
    )
    back_a = exchange(send_a)
    (send_b,) = kernel_call(
        lambda *refs: second_kernel(tail, *refs),
        [half_tiles],
        [VMEM, HBM],
        (hidden, second_all),
        [down_room, fold_room, copy_sems((rep_count,))],
        room=56,
    )
    back_b = exchange(send_b)

    later_routes, _ = lax.optimization_barrier((routes, packed))
    flat = later_routes.T.reshape(-1)
    count = flat.shape[0]
    onehot = flat[:, None] == jnp.arange(experts, dtype=jnp.int32)[None, :]
    before = jnp.arange(count)[:, None] > jnp.arange(count)[None, :]
    earlier = jnp.dot(before.astype(BF16), onehot.astype(BF16), preferred_element_type=F32)
    rank = jnp.sum(jnp.where(onehot, earlier, 0.0), axis=1).astype(jnp.int32)
    place = jnp.where(rank < HEAD, flat * HEAD + rank, experts * HEAD + flat * tail + rank - HEAD)
    place = place.reshape(top_count, tok_count)
    hit = place[:, :, None] == jnp.arange(slots, dtype=jnp.int32)[None, None, :]
    mix = jnp.sum(jnp.where(hit, route_weights.T[:, :, None], 0.0), axis=0)
    high = mix.astype(BF16)
    low = (mix - high.astype(F32)).astype(BF16)
    spare = ((0, part_rows(tok_count) - tok_count), (0, 0))
    side = projection.reshape(4, model_width // 4, unit_width).transpose(1, 0, 2).reshape(model_width // 4, -1)
    side = jnp.pad(side, ((0, 0), (0, slots - side.shape[1])))
    mix_parts = jnp.concatenate([jnp.pad(high, spare), jnp.pad(low, spare), side], axis=0)

    owner = lax.axis_index(("exp", "rep")).astype(jnp.int32)
    hit_query = jnp.max(jnp.where(positives == owner, jnp.arange(total_queries, dtype=jnp.int32), -1)).reshape(1, 1)

    (base,) = kernel_call(
        lambda *refs: mix_kernel(tail, *refs),
        [((tok_count, model_width), BF16)],
        [VMEM] * 3,
        (back_a, mix_parts, passages_in),
        [fold_room],
        room=56,
    )
    columns = query_len * total_queries
    states, states_near, weights, unit, radius, totals, logits, shares = kernel_call(
        lambda *refs: score_kernel(tail, logit_gain, *refs),
        [
            ((tok_count, model_width), BF16),
            ((tok_count, model_width), BF16),
            ((tok_count, columns), F32),
            ((tok_count, unit_width), F32),
            ((tok_count, unit_width), F32),
            ((1, columns), F32),
            ((1, total_queries), F32),
            ((2 * experts, total_queries), F32),
        ],
        [SMEM] + [VMEM] * 4,
        (hit_query, back_b, mix_parts, base, query_rows),
        [fold_room, copy_sems],
        room=24,
        out_specs=[HBM] + [VMEM] * 7,
    )

    def share_out(rows, axis):
        pairs = rows.reshape(-1, 2, total_queries)
        return lax.all_to_all(pairs, axis, split_axis=0, concat_axis=0, tiled=True).reshape(rows.shape)

    (fanned,) = kernel_call(
        lambda *refs: fan_kernel(rep_count, *refs),
        [((2 * rep_count, total_queries), F32)],
        [VMEM],
        (share_out(shares, "exp"),),
    )
    sums = share_out(fanned, "rep")
    share, loss = kernel_call(
        lambda *refs: grad_kernel(logit_gain, *refs),
        [((model_width, unit_width), BF16), ((1, LANES), F32)],
        [SMEM] + [VMEM] * 8,
        (hit_query, sums, logits, weights, totals, query_rows, unit, radius, states_near),
        room=24,
    )
    rows_out = model_width // experts
    parts = exchange(share.reshape(experts, rows_out, unit_width))
    part_sum = jnp.sum(parts.astype(F32), axis=0)
    sent = jnp.broadcast_to(part_sum[None], (rep_count,) + part_sum.shape)
    grad_projection = jnp.sum(lax.all_to_all(sent, "rep", split_axis=0, concat_axis=0, tiled=True), axis=0)
    return (states, grad_projection, loss[0, 0])


def solution(mesh):
    in_specs = (
        P(("exp", "rep"), None),
        P(("exp", "rep"), None),
        P(("exp", "rep"), None),
        P("exp", "rep", None),
        P("exp", "rep", None),
        P("exp", None, "rep"),
        P(),
        P("rep", None, None),
        P(),
    )
    out_specs = (P(("exp", "rep"), None), P("exp", None), P())
    return jax.shard_map(body, mesh=mesh, in_specs=in_specs, out_specs=out_specs, check_vma=False)
```
